32 devices in a mesh: user: 8 (over z, x), item: 4 (over y, core).
Axes of the slice: x: 2, y: 2, z: 4, core: 2. Of those that a mesh axis runs over, the one named last changes fastest.
Arguments:
- xtiles: bfloat16 [8, 96, 256, 256], P('user', 'item'), may hold values from -6 to 6
- row_bits: int32 [8, 96, 8], P('user', 'item'), may hold values from -2147483648 to 2147483646
- col_bits: int32 [8, 96, 8], P('user', 'item'), may hold values from -2147483648 to 2147483646
- tile_row: int32 [8, 96], P('user', 'item'), may hold values from 0 to 1
- tile_col: int32 [8, 96], P('user', 'item'), may hold values from 0 to 3, as said below
- tile_count: int32 [8, 4], P('user', 'item'), may hold values from 1 to 24, as said below
- user_panel: bfloat16 [4096, 256], P('user'), may hold values from -0.375 to 0.375
- item_panel: bfloat16 [1024, 256], P('item'), may hold values from -6 to 6
- test_panel: bfloat16 [1024, 256], P('item'), may hold values from -0.109375 to 0.109375
Outputs:
- sketch: float32 [4096, 256], P('user')
- second_sketch: float32 [4, 256, 256], P('item', 'user')
The draws below stay inside these ranges and needn't reach their ends.
Inputs may be any that keep to these rules, and one draw needn't show every extreme that they name: `tile_col`: the item block of slot j on user index u is j // 24 - 1, j // 24 or j // 24 + 1, taken modulo 4. `tile_count`: some device has all 24 slots live.
All inputs are finite; a program needn't handle non-finite values.
Results may differ from the reference program's by a relative error of at most 0.0022.
Values may be sent and summed in bfloat16 or wider, within the bound.
A program may use at most 64 MiB of HBM per device.

```python
import math
import jax
import jax.numpy as jnp
from jax import lax

BS = 256
K = 256
S = 256
RB = 2
TPD = 24
NU = 4096
NI = 1024
N_USER = 8
N_ITEM = 4


def draw_tile_col(key, part):
    home_block = jnp.arange(N_ITEM * TPD, dtype=jnp.int32) // TPD
    offsets = jax.random.randint(key, (N_USER, N_ITEM * TPD), -1, 2, dtype=jnp.int32)
    return (home_block[None, :] + offsets + N_ITEM) % N_ITEM


def draw_tile_count(key, part):
    first_key, second_key = jax.random.split(key)
    counts = jax.random.randint(first_key, (N_USER * N_ITEM,), 1, TPD + 1, dtype=jnp.int32)
    chosen = jax.random.randint(second_key, (), 0, N_USER * N_ITEM, dtype=jnp.int32)
    positions = jnp.arange(N_USER * N_ITEM, dtype=jnp.int32)
    counts = jnp.where(positions == chosen, TPD, counts)
    return counts.reshape(N_USER, N_ITEM)


def set_ends(values, key, smallest, largest):
    shape = values.shape
    spot = [jax.random.randint(jax.random.fold_in(key, axis), (), 0, shape[axis]) for axis in range(len(shape))]
    values = values.at[tuple(spot)].set(smallest)
    longest = shape.index(max(shape))
    spot[longest] = (spot[longest] + 1) % shape[longest]
    return values.at[tuple(spot)].set(largest)


def block_scale(own_key, shape, cuts, smallest, largest):
    gain = 1.0
    for position, blocks in cuts:
        steps = jax.random.uniform(jax.random.fold_in(jax.random.fold_in(own_key, 6), position), (blocks,), jnp.float32, smallest / len(cuts), largest / len(cuts))
        gain = gain * jnp.repeat(jnp.exp(steps), shape[position] // blocks).reshape((-1,) + (1,) * (len(shape) - 1 - position))
    return gain


def scatter_about(stream_key, dims, width, most, cuts=(), held_as=jnp.bfloat16):
    array = width * jax.random.normal(stream_key, dims, jnp.float32)
    if cuts:
        array = array * block_scale(stream_key, dims, cuts, -0.22, 0.18)
    return jnp.clip(array, -most, most).astype(held_as)


def setup_inputs(seed: int = 0) -> dict:
    streams_of = jax.random.split(jax.random.key(seed), 10)
    xtiles = scatter_about(streams_of[0], (N_USER, N_ITEM * TPD, BS, BS), 1.0, 6.0, ((0, 8), (1, 4)))
    row_bits = set_ends(jax.random.randint(streams_of[1], (N_USER, N_ITEM * TPD, BS // 32), -2147483648, 2147483647), jax.random.fold_in(streams_of[1], 1), -2147483648, 2147483646).astype(jnp.int32)
    col_bits = set_ends(jax.random.randint(streams_of[2], (N_USER, N_ITEM * TPD, BS // 32), -2147483648, 2147483647), jax.random.fold_in(streams_of[2], 1), -2147483648, 2147483646).astype(jnp.int32)
    tile_row = set_ends(jax.random.randint(streams_of[3], (N_USER, N_ITEM * TPD), 0, RB), jax.random.fold_in(streams_of[3], 1), 0, RB - 1).astype(jnp.int32)
    tile_col = draw_tile_col(jax.random.fold_in(streams_of[9], 71), 0)
    tile_count = draw_tile_count(jax.random.fold_in(streams_of[9], 71), 0)
    user_panel = scatter_about(streams_of[6], (NU, K), K ** -0.5, 0.375, ((0, 8),))
    item_panel = scatter_about(streams_of[7], (NI, K), 1.0, 6.0, ((0, 4),))
    test_panel = scatter_about(streams_of[8], (NI, S), (N_ITEM * TPD * BS // (4 * RB)) ** -0.5, 0.109375, ((0, 4),))
    return dict(xtiles=xtiles, row_bits=row_bits, col_bits=col_bits, tile_row=tile_row, tile_col=tile_col, tile_count=tile_count, user_panel=user_panel, item_panel=item_panel, test_panel=test_panel)


def unpack(packed):
    offsets = jnp.arange(32, dtype=jnp.int32)
    bit_values = jnp.right_shift(packed[..., None], offsets) & 1
    return bit_values.reshape(packed.shape[:-1] + (packed.shape[-1] * 32,)).astype(jnp.float32)

def reference(xtiles, row_bits, col_bits, tile_row, tile_col, tile_count, user_panel, item_panel, test_panel):
    user_blocks = user_panel.reshape(N_USER, RB, BS, K)
    item_blocks = item_panel.reshape(N_ITEM, BS, K).astype(jnp.float32)
    test_blocks = test_panel.reshape(N_ITEM, BS, S).astype(jnp.float32)
    slot_ids = jnp.arange(N_ITEM * TPD, dtype=jnp.int32)

    def residual_rows(inputs):
        tile_data, row_packed, col_packed, row_ids, col_ids, counts, user_rows = inputs
        live_slots = (slot_ids % TPD < counts[slot_ids // TPD]).astype(jnp.float32)
        observed = unpack(row_packed)[:, :, None] * unpack(col_packed)[:, None, :] * live_slots[:, None, None]
        predicted = jnp.einsum('tak,tbk->tab', user_rows[row_ids].astype(jnp.float32), item_blocks[col_ids])
        residue = (observed * (tile_data.astype(jnp.float32) - predicted)).astype(jnp.bfloat16)
        sketch_tiles = jnp.einsum('tab,tbs->tas', residue.astype(jnp.float32), test_blocks[col_ids])
        return (residue, jax.ops.segment_sum(sketch_tiles, row_ids, num_segments=RB))
    residue, sketch = lax.map(residual_rows, (xtiles, row_bits, col_bits, tile_row, tile_col, tile_count, user_blocks))
    sketch_half = sketch.astype(jnp.bfloat16)

    def column_sums(running, inputs):
        residue_user, row_ids, col_ids, sketch_user = inputs
        column_tiles = jnp.einsum('tab,tas->tbs', residue_user.astype(jnp.float32), sketch_user[row_ids].astype(jnp.float32))
        return (running + jax.ops.segment_sum(column_tiles, col_ids, num_segments=N_ITEM), None)
    zero_sums = jnp.zeros((N_ITEM, BS, S), jnp.float32)
    running, _ = lax.scan(column_sums, zero_sums, (residue, tile_row, tile_col, sketch_half))
    sketch_scale = 2.0 / math.sqrt(N_USER * TPD * BS)
    return (sketch.reshape(N_USER * RB * BS, S), running * sketch_scale)
```

```python
import functools
import math

import jax
import jax.numpy as jnp
from jax import lax
from jax.experimental import pallas as pl
from jax.experimental.pallas import tpu as pltpu
from jax.sharding import PartitionSpec as P

MESH = pl.DeviceIdType.MESH
F32 = jnp.float32
BF16 = jnp.bfloat16
CHUNKS = 4


def sorting_pairs(length):
    size = 1 << (length - 1).bit_length()
    pairs = []
    p = 1
    while p < size:
        k = p
        while k >= 1:
            for j in range(k % p, size - k, 2 * k):
                for i in range(min(k, size - j - k)):
                    if (i + j) // (2 * p) == (i + j + k) // (2 * p):
                        pairs.append((i + j, i + j + k))
            k //= 2
        p *= 2
    return [(a, b) for a, b in pairs if b < length]


def kernel(
    n_user,
    n_item,
    scale,
    row_bits,
    col_bits,
    tile_row,
    tile_col,
    tile_count,
    user_ref,
    x_hbm,
    item_hbm,
    test_hbm,
    sketch_out,
    second_out,
    x_buf,
    v_all,
    t_all,
    p_buf,
    prefix,
    keys,
    a_hi,
    a_lo,
    at_hi,
    at_lo,
    half_send,
    half_recv,
    own_half,
    gathered,
    y_full,
    z_send,
    z_recv,
    z_own,
    piece_own,
    piece_send,
    piece_recv,
    local_sem,
    panel_send_sem,
    panel_recv_sem,
    half_send_sem,
    half_recv_sem,
    chip_send_sem,
    chip_recv_sem,
    y_send_sem,
    y_recv_sem,
    z_send_sem,
    z_recv_sem,
    piece_send_sem,
    piece_recv_sem,
):
    user = lax.axis_index("user")
    item = lax.axis_index("item")
    core = lax.rem(item, 2)
    chip = item // 2
    chips = n_item // 2
    slots, size = x_buf.shape[0], x_buf.shape[1]
    blocks = user_ref.shape[0] // size
    lower = lax.rem(item + n_item - 1, n_item)
    upper = lax.rem(item + 1, n_item)
    partner = chip * 2 + 1 - core
    far_window = 2 * core
    near_window = 2 - far_window
    far_item = jnp.where(core == 0, lower, upper)

    x_copy = pltpu.make_async_copy(x_hbm.at[0], x_buf, local_sem.at[0])
    v_copy = pltpu.make_async_copy(item_hbm, v_all.at[1], local_sem.at[1])
    t_copy = pltpu.make_async_copy(test_hbm, t_all.at[1], local_sem.at[2])
    v_copy.start()
    x_copy.start()
    t_copy.start()

    barrier = pltpu.get_barrier_semaphore()
    pl.semaphore_signal(barrier, inc=1, device_id={"item": far_item}, device_id_type=MESH)
    pl.semaphore_signal(barrier, inc=1, device_id={"item": partner}, device_id_type=MESH)
    for d in range(1, chips):
        other = lax.rem(chip + d, chips) * 2 + core
        pl.semaphore_signal(barrier, inc=1, device_id={"item": other}, device_id_type=MESH)
    for d in range(1, n_user):
        pl.semaphore_signal(
            barrier, inc=1, device_id={"user": lax.rem(user + d, n_user)}, device_id_type=MESH
        )
    pl.semaphore_wait(barrier, 2 + (chips - 1) + (n_user - 1))

    panel_copies = []
    for which, (source, target) in enumerate(((item_hbm, v_all), (test_hbm, t_all))):
        for side, (window, device) in enumerate(((near_window, far_item), (far_window, partner))):
            panel_copies.append(
                pltpu.make_async_remote_copy(
                    src_ref=source,
                    dst_ref=target.at[window],
                    send_sem=panel_send_sem.at[which, side],
                    recv_sem=panel_recv_sem.at[which, side],
                    device_id={"item": device},
                    device_id_type=MESH,
                )
            )
            panel_copies[-1].start()

    stride = 1 << (slots - 1).bit_length()
    order = []
    for t in range(slots):
        window = lax.rem(tile_col[0, t] - item + 1 + n_item, n_item)
        order.append((tile_row[0, t] * 3 + window) * stride + t)
    for a, b in sorting_pairs(slots):
        order[a], order[b] = jnp.minimum(order[a], order[b]), jnp.maximum(order[a], order[b])
    for t in range(slots):
        keys[t] = order[t]
    bounds = []
    for group in range(blocks * 3 + 1):
        bounds.append(sum((key < group * stride).astype(jnp.int32) for key in order))

    def predict(window):
        product = lax.dot_general(
            user_ref[...], v_all[window], (((1,), (1,)), ((), ())), preferred_element_type=F32
        )
        for r in range(blocks):
            p_buf[r * 3 + window] = product[r * size : (r + 1) * size]

    v_copy.wait()
    predict(1)
    prefix[0] = jnp.zeros((size, size), F32)
    panel_copies[1].wait_recv()
    panel_copies[0].wait_recv()
    predict(0)
    predict(2)
    x_copy.wait()

    strip = 16
    lanes = lax.broadcasted_iota(jnp.int32, (strip, size), 1)
    rows = lax.broadcasted_iota(jnp.int32, (strip, size), 0)

    def add_tile(i, carry):
        key = keys[i]
        t = jnp.bitwise_and(key, stride - 1)
        group = lax.shift_right_logical(key, stride.bit_length() - 1)
        live = (t < tile_count[0, 0]).astype(jnp.int32)
        words = jnp.zeros((strip, size), jnp.int32)
        for w in range(size // 32):
            words = jnp.where(lanes // 32 == w, col_bits[0, t, w] * live, words)
        col_seen = jnp.bitwise_and(lax.shift_right_logical(words, jnp.bitwise_and(lanes, 31)), 1)
        for s in range(size // strip):
            at = slice(s * strip, (s + 1) * strip)
            word = jnp.full((strip, size), row_bits[0, t, s * strip // 32], jnp.int32)
            seen = jnp.bitwise_and(
                lax.shift_right_logical(word, rows + (s * strip) % 32), col_seen
            )
            gap = x_buf[t, at, :].astype(F32) - p_buf[group, at, :]
            residue = jnp.where(seen != 0, gap, 0.0).astype(BF16)
            prefix[i + 1, at, :] = prefix[i, at, :] + residue.astype(F32)
        return carry

    lax.fori_loop(0, slots, add_tile, 0)

    for r in range(blocks):
        for window in range(3):
            group = r * 3 + window
            total = prefix[bounds[group + 1]] - prefix[bounds[group]]
            high = total.astype(BF16)
            a_hi[r, window] = high
            a_lo[r, window] = (total - high.astype(F32)).astype(BF16)
    t_copy.wait()
    panel_copies[3].wait_recv()
    panel_copies[2].wait_recv()

    def sketch_block(r):
        total = None
        for window in range(3):
            for part in (a_hi, a_lo):
                term = jnp.dot(part[r, window], t_all[window], preferred_element_type=F32)
                total = term if total is None else total + term
        return total

    step = size // CHUNKS
    half_send[...] = sketch_block(1 - core)
    half_copies = []
    for j in range(CHUNKS):
        at = pl.ds(j * step, step)
        half_copies.append(
            pltpu.make_async_remote_copy(
                src_ref=half_send.at[at],
                dst_ref=half_recv.at[at],
                send_sem=half_send_sem.at[j],
                recv_sem=half_recv_sem.at[j],
                device_id={"item": partner},
                device_id_type=MESH,
            )
        )
        half_copies[-1].start()
    own_half[...] = sketch_block(core)

    chip_copies = []
    for j in range(CHUNKS):
        at = pl.ds(j * step, step)
        half_copies[j].wait_recv()
        gathered[chip, at, :] = own_half[at, :] + half_recv[at, :]
        for d in range(1, chips):
            chip_copies.append(
                pltpu.make_async_remote_copy(
                    src_ref=gathered.at[chip, at],
                    dst_ref=gathered.at[chip, at],
                    send_sem=chip_send_sem.at[j, d - 1],
                    recv_sem=chip_recv_sem.at[j, d - 1],
                    device_id={"item": lax.rem(chip + d, chips) * 2 + core},
                    device_id_type=MESH,
                )
            )
            chip_copies[-1].start()

    for r in range(blocks):
        for window in range(3):
            group = r * 3 + window
            turned = (prefix[bounds[group + 1]] - prefix[bounds[group]]).T
            high = turned.astype(BF16)
            at_hi[window, :, r * size : (r + 1) * size] = high
            at_lo[window, :, r * size : (r + 1) * size] = (turned - high.astype(F32)).astype(BF16)

    y_copies = []
    for j in range(CHUNKS):
        at = pl.ds(j * step, step)
        for d in range(1, chips):
            chip_copies[j * (chips - 1) + d - 1].wait_recv()
        total = gathered[0, at, :]
        for other in range(1, chips):
            total = total + gathered[other, at, :]
        y_full[core, at, :] = total
        y_copies.append(
            pltpu.make_async_remote_copy(
                src_ref=y_full.at[core, at],
                dst_ref=y_full.at[core, at],
                send_sem=y_send_sem.at[j],
                recv_sem=y_recv_sem.at[j],
                device_id={"item": partner},
                device_id_type=MESH,
            )
        )
        y_copies[-1].start()
    for j in range(CHUNKS):
        y_copies[j].wait_recv()
    out_copy = pltpu.make_async_copy(y_full, sketch_out, local_sem.at[3])
    out_copy.start()
    y_half = y_full[...].astype(BF16).reshape(blocks * size, size)

    def second(window):
        return jnp.dot(at_hi[window], y_half, preferred_element_type=F32) + jnp.dot(
            at_lo[window], y_half, preferred_element_type=F32
        )

    piece = size // n_user
    turns = sorted(range(1, n_user), key=lambda d: -min(d, n_user - d)) + [0]
    z_copies = [[], []]
    for side, (window, facing, device) in enumerate(
        ((far_window, near_window, far_item), (near_window, far_window, partner))
    ):
        z_send[side] = second(window).astype(z_send.dtype).reshape(n_user, piece, size)
        for n, d in enumerate(turns):
            target = lax.rem(user + d, n_user)
            z_copies[side].append(
                pltpu.make_async_remote_copy(
                    src_ref=z_send.at[side, target],
                    dst_ref=z_recv.at[side, target],
                    send_sem=z_send_sem.at[side, n],
                    recv_sem=z_recv_sem.at[side, n],
                    device_id={"item": device},
                    device_id_type=MESH,
                )
            )
            z_copies[side][-1].start()
    z_own[...] = second(1).reshape(n_user, piece, size)

    piece_copies = []
    for n, d in enumerate(turns):
        target = lax.rem(user + d, n_user)
        z_copies[1][n].wait_recv()
        z_copies[0][n].wait_recv()
        total = z_own[target] + z_recv[0, target].astype(F32) + z_recv[1, target].astype(F32)
        if d == 0:
            piece_own[...] = total
            continue
        piece_send[target] = total.astype(piece_send.dtype)
        piece_copies.append(
            pltpu.make_async_remote_copy(
                src_ref=piece_send.at[target],
                dst_ref=piece_recv.at[n],
                send_sem=piece_send_sem.at[n],
                recv_sem=piece_recv_sem.at[n],
                device_id={"user": target},
                device_id_type=MESH,
            )
        )
        piece_copies[-1].start()
    total = piece_own[...]
    for n, copy in enumerate(piece_copies):
        copy.wait_recv()
        total = total + piece_recv[n].astype(F32)
    second_out[0] = total * scale

    out_copy.wait()
    for copy in panel_copies + half_copies + chip_copies + y_copies + z_copies[0] + z_copies[1]:
        copy.wait_send()
    for copy in piece_copies:
        copy.wait_send()


def shards(
    xtiles, row_bits, col_bits, tile_row, tile_col, tile_count, user_panel, item_panel, test_panel
):
    size = item_panel.shape[0]
    slots = xtiles.shape[1]
    blocks = user_panel.shape[0] // size
    n_user, n_item = lax.axis_size("user"), lax.axis_size("item")
    chips = n_item // 2
    piece = size // n_user
    sent = BF16 if piece % 16 == 0 else F32
    scale = 2.0 / math.sqrt(n_user * slots * size)
    square = (size, size)
    dma = pltpu.SemaphoreType.DMA
    smem = pl.BlockSpec(memory_space=pltpu.SMEM)
    vmem = pl.BlockSpec(memory_space=pltpu.VMEM)
    hbm = pl.BlockSpec(memory_space=pl.ANY)
    sketch, second = pl.pallas_call(
        functools.partial(kernel, n_user, n_item, scale),
        out_shape=(
            jax.ShapeDtypeStruct((blocks,) + square, F32),
            jax.ShapeDtypeStruct((1, piece, size), F32),
        ),
        in_specs=[smem] * 5 + [vmem] + [hbm] * 3,
        out_specs=(hbm, vmem),
        scratch_shapes=[
            pltpu.VMEM((slots,) + square, BF16),
            pltpu.VMEM((3,) + square, BF16),
            pltpu.VMEM((3,) + square, BF16),
            pltpu.VMEM((blocks * 3,) + square, F32),
            pltpu.VMEM((slots + 1,) + square, F32),
            pltpu.SMEM((slots,), jnp.int32),
            pltpu.VMEM((blocks, 3) + square, BF16),
            pltpu.VMEM((blocks, 3) + square, BF16),
            pltpu.VMEM((3, size, blocks * size), BF16),
            pltpu.VMEM((3, size, blocks * size), BF16),
            pltpu.VMEM(square, F32),
            pltpu.VMEM(square, F32),
            pltpu.VMEM(square, F32),
            pltpu.VMEM((chips,) + square, F32),
            pltpu.VMEM((blocks,) + square, F32),
            pltpu.VMEM((2, n_user, piece, size), sent),
            pltpu.VMEM((2, n_user, piece, size), sent),
            pltpu.VMEM((n_user, piece, size), F32),
            pltpu.VMEM((piece, size), F32),
            pltpu.VMEM((n_user, piece, size), sent),
            pltpu.VMEM((n_user - 1, piece, size), sent),
            dma((4,)),
            dma((2, 2)),
            dma((2, 2)),
            dma((CHUNKS,)),
            dma((CHUNKS,)),
            dma((CHUNKS, chips - 1)),
            dma((CHUNKS, chips - 1)),
            dma((CHUNKS,)),
            dma((CHUNKS,)),
            dma((2, n_user)),
            dma((2, n_user)),
            dma((n_user - 1,)),
            dma((n_user - 1,)),
        ],
        compiler_params=pltpu.CompilerParams(
            collective_id=0, has_side_effects=True, vmem_limit_bytes=48 * 1024 * 1024
        ),
    )(
        row_bits,
        col_bits,
        tile_row,
        tile_col,
        tile_count,
        user_panel,
        xtiles,
        item_panel,
        test_panel,
    )
    return sketch.reshape(blocks * size, size), second


def solution(mesh):
    placed = (
        P("user", "item", None, None),
        P("user", "item", None),
        P("user", "item", None),
        P("user", "item"),
        P("user", "item"),
        P("user", "item"),
        P("user", None),
        P("item", None),
        P("item", None),
    )
    return jax.shard_map(
        shards,
        mesh=mesh,
        in_specs=placed,
        out_specs=(P("user", None), P("item", "user", None)),
        check_vma=False,
    )
```

```python
import functools
import math

import jax
import jax.numpy as jnp
from jax import lax
from jax.experimental import pallas as pl
from jax.experimental.pallas import tpu as pltpu
from jax.sharding import PartitionSpec as P

MESH = pl.DeviceIdType.MESH
F32 = jnp.float32
BF16 = jnp.bfloat16
CHUNKS = 4


def sorting_pairs(length):
    size = 1 << (length - 1).bit_length()
    pairs = []
    p = 1
    while p < size:
        k = p
        while k >= 1:
            for j in range(k % p, size - k, 2 * k):
                for i in range(min(k, size - j - k)):
                    if (i + j) // (2 * p) == (i + j + k) // (2 * p):
                        pairs.append((i + j, i + j + k))
            k //= 2
        p *= 2
    return [(a, b) for a, b in pairs if b < length]


def kernel(
    n_user,
    n_item,
    scale,
    row_bits_hbm,
    col_bits_hbm,
    tile_row_hbm,
    tile_col_hbm,
    tile_count_hbm,
    user_hbm,
    x_hbm,
    item_hbm,
    test_hbm,
    sketch_out,
    second_out,
    row_bits,
    col_bits,
    tile_row,
    tile_col,
    tile_count,
    user_ref,
    x_buf,
    masks,
    v_all,
    t_all,
    p_buf,
    prefix,
    keys,
    a_hi,
    a_lo,
    at_hi,
    at_lo,
    half_send,
    half_recv,
    own_half,
    gathered,
    y_full,
    z_send,
    z_recv,
    z_own,
    piece_own,
    piece_send,
    piece_recv,
    local_sem,
    panel_send_sem,
    panel_recv_sem,
    half_send_sem,
    half_recv_sem,
    chip_send_sem,
    chip_recv_sem,
    y_send_sem,
    y_recv_sem,
    z_send_sem,
    z_recv_sem,
    piece_send_sem,
    piece_recv_sem,
):
    user = lax.axis_index("user")
    item = lax.axis_index("item")
    core = lax.rem(item, 2)
    chip = item // 2
    chips = n_item // 2
    slots, size = x_buf.shape[0], x_buf.shape[1]
    blocks = user_ref.shape[0] // size
    lower = lax.rem(item + n_item - 1, n_item)
    upper = lax.rem(item + 1, n_item)
    partner = chip * 2 + 1 - core
    far_window = 2 * core
    near_window = 2 - far_window
    far_item = jnp.where(core == 0, lower, upper)

    x_copy = pltpu.make_async_copy(x_hbm.at[0], x_buf, local_sem.at[0])
    v_copy = pltpu.make_async_copy(item_hbm, v_all.at[1], local_sem.at[1])
    t_copy = pltpu.make_async_copy(test_hbm, t_all.at[1], local_sem.at[2])
    u_copy = pltpu.make_async_copy(user_hbm, user_ref, local_sem.at[4])
    small_copies = [
        pltpu.make_async_copy(source, target, local_sem.at[5 + n])
        for n, (source, target) in enumerate(
            (
                (tile_row_hbm, tile_row),
                (tile_col_hbm, tile_col),
                (tile_count_hbm, tile_count),
                (row_bits_hbm, row_bits),
                (col_bits_hbm, col_bits),
            )
        )
    ]
    for copy in small_copies + [u_copy, v_copy, x_copy, t_copy]:
        copy.start()

    barrier = pltpu.get_barrier_semaphore()
    pl.semaphore_signal(barrier, inc=1, device_id={"item": far_item}, device_id_type=MESH)
    pl.semaphore_signal(barrier, inc=1, device_id={"item": partner}, device_id_type=MESH)
    for d in range(1, chips):
        other = lax.rem(chip + d, chips) * 2 + core
        pl.semaphore_signal(barrier, inc=1, device_id={"item": other}, device_id_type=MESH)
    for d in range(1, n_user):
        pl.semaphore_signal(
            barrier, inc=1, device_id={"user": lax.rem(user + d, n_user)}, device_id_type=MESH
        )
    pl.semaphore_wait(barrier, 2 + (chips - 1) + (n_user - 1))

    panel_copies = []
    for which, (source, target) in enumerate(((item_hbm, v_all), (test_hbm, t_all))):
        for side, (window, device) in enumerate(((near_window, far_item), (far_window, partner))):
            panel_copies.append(
                pltpu.make_async_remote_copy(
                    src_ref=source,
                    dst_ref=target.at[window],
                    send_sem=panel_send_sem.at[which, side],
                    recv_sem=panel_recv_sem.at[which, side],
                    device_id={"item": device},
                    device_id_type=MESH,
                )
            )
            panel_copies[-1].start()

    for copy in small_copies:
        copy.wait()
    strip = 16
    lanes = lax.broadcasted_iota(jnp.int32, (strip, size), 1)
    rows = lax.broadcasted_iota(jnp.int32, (strip, size), 0)

    def make_mask(t, carry):
        live = (t < tile_count[0, 0]).astype(jnp.int32)
        words = jnp.zeros((strip, size), jnp.int32)
        for w in range(size // 32):
            words = jnp.where(lanes // 32 == w, col_bits[0, w, t] * live, words)
        col_seen = jnp.bitwise_and(lax.shift_right_logical(words, jnp.bitwise_and(lanes, 31)), 1)
        for s in range(size // strip):
            word = jnp.full((strip, size), row_bits[0, s * strip // 32, t], jnp.int32)
            seen = jnp.bitwise_and(
                lax.shift_right_logical(word, rows + (s * strip) % 32), col_seen
            )
            masks[t, s * strip : (s + 1) * strip, :] = seen.astype(F32).astype(BF16)
        return carry

    lax.fori_loop(0, slots, make_mask, 0)

    stride = 1 << (slots - 1).bit_length()
    order = []
    for t in range(slots):
        window = lax.rem(tile_col[0, t] - item + 1 + n_item, n_item)
        order.append((tile_row[0, t] * 3 + window) * stride + t)
    for a, b in sorting_pairs(slots):
        order[a], order[b] = jnp.minimum(order[a], order[b]), jnp.maximum(order[a], order[b])
    for t in range(slots):
        keys[t] = order[t]
    bounds = []
    for group in range(blocks * 3 + 1):
        bounds.append(sum((key < group * stride).astype(jnp.int32) for key in order))

    def predict(window):
        product = lax.dot_general(
            user_ref[...], v_all[window], (((1,), (1,)), ((), ())), preferred_element_type=F32
        )
        for r in range(blocks):
            p_buf[r * 3 + window] = product[r * size : (r + 1) * size]

    prefix[0] = jnp.zeros((size, size), F32)
    u_copy.wait()
    v_copy.wait()
    predict(1)
    panel_copies[1].wait_recv()
    predict(near_window)
    x_copy.wait()
    panel_copies[0].wait_recv()
    predict(far_window)

    def add_tile(i, carry):
        key = keys[i]
        t = jnp.bitwise_and(key, stride - 1)
        group = lax.shift_right_logical(key, stride.bit_length() - 1)
        for s in range(size // strip):
            at = slice(s * strip, (s + 1) * strip)
            gap = x_buf[t, at, :].astype(F32) - p_buf[group, at, :]
            residue = gap.astype(BF16) * masks[t, at, :]
            prefix[i + 1, at, :] = prefix[i, at, :] + residue.astype(F32)
        return carry

    lax.fori_loop(0, slots, add_tile, 0)

    for r in range(blocks):
        for window in range(3):
            group = r * 3 + window
            total = prefix[bounds[group + 1]] - prefix[bounds[group]]
            high = total.astype(BF16)
            a_hi[r, window] = high
            a_lo[r, window] = (total - high.astype(F32)).astype(BF16)
    t_copy.wait()
    panel_copies[3].wait_recv()
    panel_copies[2].wait_recv()

    def sketch_block(r):
        total = None
        for window in range(3):
            for part in (a_hi, a_lo):
                term = jnp.dot(part[r, window], t_all[window], preferred_element_type=F32)
                total = term if total is None else total + term
        return total

    step = size // CHUNKS
    half_send[...] = sketch_block(1 - core)
    half_copies = []
    for j in range(CHUNKS):
        at = pl.ds(j * step, step)
        half_copies.append(
            pltpu.make_async_remote_copy(
                src_ref=half_send.at[at],
                dst_ref=half_recv.at[at],
                send_sem=half_send_sem.at[j],
                recv_sem=half_recv_sem.at[j],
                device_id={"item": partner},
                device_id_type=MESH,
            )
        )
        half_copies[-1].start()
    own_half[...] = sketch_block(core)

    chip_copies = []
    for j in range(CHUNKS):
        at = pl.ds(j * step, step)
        half_copies[j].wait_recv()
        gathered[chip, at, :] = own_half[at, :] + half_recv[at, :]
        for d in range(1, chips):
            chip_copies.append(
                pltpu.make_async_remote_copy(
                    src_ref=gathered.at[chip, at],
                    dst_ref=gathered.at[chip, at],
                    send_sem=chip_send_sem.at[j, d - 1],
                    recv_sem=chip_recv_sem.at[j, d - 1],
                    device_id={"item": lax.rem(chip + d, chips) * 2 + core},
                    device_id_type=MESH,
                )
            )
            chip_copies[-1].start()

    for r in range(blocks):
        for window in range(3):
            group = r * 3 + window
            turned = (prefix[bounds[group + 1]] - prefix[bounds[group]]).T
            high = turned.astype(BF16)
            at_hi[window, :, r * size : (r + 1) * size] = high
            at_lo[window, :, r * size : (r + 1) * size] = (turned - high.astype(F32)).astype(BF16)

    y_copies = []
    for j in range(CHUNKS):
        at = pl.ds(j * step, step)
        for d in range(1, chips):
            chip_copies[j * (chips - 1) + d - 1].wait_recv()
        total = gathered[0, at, :]
        for other in range(1, chips):
            total = total + gathered[other, at, :]
        y_full[core, at, :] = total
        y_copies.append(
            pltpu.make_async_remote_copy(
                src_ref=y_full.at[core, at],
                dst_ref=y_full.at[core, at],
                send_sem=y_send_sem.at[j],
                recv_sem=y_recv_sem.at[j],
                device_id={"item": partner},
                device_id_type=MESH,
            )
        )
        y_copies[-1].start()
    for j in range(CHUNKS):
        y_copies[j].wait_recv()
    out_copy = pltpu.make_async_copy(y_full, sketch_out, local_sem.at[3])
    out_copy.start()
    y_half = y_full[...].astype(BF16).reshape(blocks * size, size)

    def second(window):
        return jnp.dot(at_hi[window], y_half, preferred_element_type=F32) + jnp.dot(
            at_lo[window], y_half, preferred_element_type=F32
        )

    piece = size // n_user
    turns = sorted(range(1, n_user), key=lambda d: -min(d, n_user - d)) + [0]
    z_copies = [[], []]
    for side, (window, facing, device) in enumerate(
        ((far_window, near_window, far_item), (near_window, far_window, partner))
    ):
        z_send[side] = second(window).astype(z_send.dtype).reshape(n_user, piece, size)
        for n, d in enumerate(turns):
            target = lax.rem(user + d, n_user)
            z_copies[side].append(
                pltpu.make_async_remote_copy(
                    src_ref=z_send.at[side, target],
                    dst_ref=z_recv.at[side, target],
                    send_sem=z_send_sem.at[side, n],
                    recv_sem=z_recv_sem.at[side, n],
                    device_id={"item": device},
                    device_id_type=MESH,
                )
            )
            z_copies[side][-1].start()
    z_own[...] = second(1).reshape(n_user, piece, size)

    piece_copies = []
    for n, d in enumerate(turns):
        target = lax.rem(user + d, n_user)
        z_copies[1][n].wait_recv()
        z_copies[0][n].wait_recv()
        total = z_own[target] + z_recv[0, target].astype(F32) + z_recv[1, target].astype(F32)
        if d == 0:
            piece_own[...] = total
            continue
        piece_send[target] = total.astype(piece_send.dtype)
        piece_copies.append(
            pltpu.make_async_remote_copy(
                src_ref=piece_send.at[target],
                dst_ref=piece_recv.at[n],
                send_sem=piece_send_sem.at[n],
                recv_sem=piece_recv_sem.at[n],
                device_id={"user": target},
                device_id_type=MESH,
            )
        )
        piece_copies[-1].start()
    total = piece_own[...]
    for n, copy in enumerate(piece_copies):
        copy.wait_recv()
        total = total + piece_recv[n].astype(F32)
    second_out[0] = total * scale

    out_copy.wait()
    for copy in panel_copies + half_copies + chip_copies + y_copies + z_copies[0] + z_copies[1]:
        copy.wait_send()
    for copy in piece_copies:
        copy.wait_send()


def hand_over(sketch, second, sketch_out, second_out, sem):
    copies = [pltpu.make_async_copy(second, second_out, sem.at[0])]
    for r in range(sketch.shape[0]):
        copies.append(pltpu.make_async_copy(sketch.at[r], sketch_out.at[r], sem.at[1 + r]))
    for copy in copies:
        copy.start()
    for copy in copies:
        copy.wait()


def shards(
    xtiles, row_bits, col_bits, tile_row, tile_col, tile_count, user_panel, item_panel, test_panel
):
    size = item_panel.shape[0]
    slots = xtiles.shape[1]
    blocks = user_panel.shape[0] // size
    n_user, n_item = lax.axis_size("user"), lax.axis_size("item")
    chips = n_item // 2
    piece = size // n_user
    sent = BF16 if piece % 16 == 0 else F32
    scale = 2.0 / math.sqrt(n_user * slots * size)
    square = (size, size)
    words = row_bits.shape[2]
    dma = pltpu.SemaphoreType.DMA
    vmem = pl.BlockSpec(memory_space=pltpu.VMEM)
    hbm = pl.BlockSpec(memory_space=pltpu.HBM)
    sketch, second = pl.pallas_call(
        functools.partial(kernel, n_user, n_item, scale),
        out_shape=(
            jax.ShapeDtypeStruct((blocks,) + square, F32),
            jax.ShapeDtypeStruct((1, piece, size), F32),
        ),
        in_specs=[hbm] * 9,
        out_specs=(hbm, vmem),
        scratch_shapes=[
            pltpu.SMEM((1, words, slots), jnp.int32),
            pltpu.SMEM((1, words, slots), jnp.int32),
            pltpu.SMEM((1, slots), jnp.int32),
            pltpu.SMEM((1, slots), jnp.int32),
            pltpu.SMEM((1, 1), jnp.int32),
            pltpu.VMEM(user_panel.shape, BF16),
            pltpu.VMEM((slots,) + square, BF16),
            pltpu.VMEM((slots,) + square, BF16),
            pltpu.VMEM((3,) + square, BF16),
            pltpu.VMEM((3,) + square, BF16),
            pltpu.VMEM((blocks * 3,) + square, F32),
            pltpu.VMEM((slots + 1,) + square, F32),
            pltpu.SMEM((slots,), jnp.int32),
            pltpu.VMEM((blocks, 3) + square, BF16),
            pltpu.VMEM((blocks, 3) + square, BF16),
            pltpu.VMEM((3, size, blocks * size), BF16),
            pltpu.VMEM((3, size, blocks * size), BF16),
            pltpu.VMEM(square, F32),
            pltpu.VMEM(square, F32),
            pltpu.VMEM(square, F32),
            pltpu.VMEM((chips,) + square, F32),
            pltpu.VMEM((blocks,) + square, F32),
            pltpu.VMEM((2, n_user, piece, size), sent),
            pltpu.VMEM((2, n_user, piece, size), sent),
            pltpu.VMEM((n_user, piece, size), F32),
            pltpu.VMEM((piece, size), F32),
            pltpu.VMEM((n_user, piece, size), sent),
            pltpu.VMEM((n_user - 1, piece, size), sent),
            dma((10,)),
            dma((2, 2)),
            dma((2, 2)),
            dma((CHUNKS,)),
            dma((CHUNKS,)),
            dma((CHUNKS, chips - 1)),
            dma((CHUNKS, chips - 1)),
            dma((CHUNKS,)),
            dma((CHUNKS,)),
            dma((2, n_user)),
            dma((2, n_user)),
            dma((n_user - 1,)),
            dma((n_user - 1,)),
        ],
        compiler_params=pltpu.CompilerParams(
            collective_id=0, has_side_effects=True, vmem_limit_bytes=63 * 1024 * 1024
        ),
    )(
        jnp.swapaxes(row_bits, 1, 2),
        jnp.swapaxes(col_bits, 1, 2),
        tile_row,
        tile_col,
        tile_count,
        user_panel,
        xtiles,
        item_panel,
        test_panel,
    )
    sketch, second = pl.pallas_call(
        hand_over,
        out_shape=(
            jax.ShapeDtypeStruct(sketch.shape, F32),
            jax.ShapeDtypeStruct(second.shape, F32),
        ),
        in_specs=[hbm] * 2,
        out_specs=(hbm, hbm),
        scratch_shapes=[dma((blocks + 1,))],
        compiler_params=pltpu.CompilerParams(vmem_limit_bytes=63 * 1024 * 1024),
    )(sketch, second)
    return sketch.reshape(blocks * size, size), second


def solution(mesh):
    placed = (
        P("user", "item", None, None),
        P("user", "item", None),
        P("user", "item", None),
        P("user", "item"),
        P("user", "item"),
        P("user", "item"),
        P("user", None),
        P("item", None),
        P("item", None),
    )
    return jax.shard_map(
        shards,
        mesh=mesh,
        in_specs=placed,
        out_specs=(P("user", None), P("item", "user", None)),
        check_vma=False,
    )
```

```python
import functools
import math

import jax
import jax.numpy as jnp
from jax import lax
from jax.experimental import pallas as pl
from jax.experimental.pallas import tpu as pltpu
from jax.sharding import PartitionSpec as P

MESH = pl.DeviceIdType.MESH
F32 = jnp.float32
BF16 = jnp.bfloat16
CHUNKS = 4


def sorting_pairs(length):
    size = 1 << (length - 1).bit_length()
    pairs = []
    p = 1
    while p < size:
        k = p
        while k >= 1:
            for j in range(k % p, size - k, 2 * k):
                for i in range(min(k, size - j - k)):
                    if (i + j) // (2 * p) == (i + j + k) // (2 * p):
                        pairs.append((i + j, i + j + k))
            k //= 2
        p *= 2
    return [(a, b) for a, b in pairs if b < length]


def kernel(
    n_user,
    n_item,
    scale,
    row_bits_hbm,
    col_bits_hbm,
    tile_row_hbm,
    tile_col_hbm,
    tile_count_hbm,
    user_hbm,
    x_hbm,
    item_hbm,
    test_hbm,
    sketch_out,
    second_out,
    row_bits,
    col_bits,
    tile_row,
    tile_col,
    tile_count,
    user_ref,
    x_buf,
    masks,
    v_all,
    t_all,
    p_buf,
    prefix,
    keys,
    bounds,
    a_hi,
    a_lo,
    at_hi,
    at_lo,
    half_send,
    half_recv,
    own_half,
    gathered,
    y_full,
    z_part,
    far_send,
    far_recv,
    near_send,
    near_recv,
    z_own,
    piece_own,
    piece_send,
    piece_recv,
    local_sem,
    panel_send_sem,
    panel_recv_sem,
    half_send_sem,
    half_recv_sem,
    chip_send_sem,
    chip_recv_sem,
    y_send_sem,
    y_recv_sem,
    z_send_sem,
    z_recv_sem,
    piece_send_sem,
    piece_recv_sem,
):
    user = lax.axis_index("user")
    item = lax.axis_index("item")
    core = lax.rem(item, 2)
    chip = item // 2
    chips = n_item // 2
    slots, size = x_buf.shape[0], x_buf.shape[1]
    blocks = user_ref.shape[0] // size
    lower = lax.rem(item + n_item - 1, n_item)
    upper = lax.rem(item + 1, n_item)
    partner = chip * 2 + 1 - core
    far_window = 2 * core
    near_window = 2 - far_window
    far_item = jnp.where(core == 0, lower, upper)

    x_copy = pltpu.make_async_copy(x_hbm.at[0], x_buf, local_sem.at[0])
    v_copy = pltpu.make_async_copy(item_hbm, v_all.at[1], local_sem.at[1])
    t_copy = pltpu.make_async_copy(test_hbm, t_all.at[1], local_sem.at[2])
    u_copy = pltpu.make_async_copy(user_hbm, user_ref, local_sem.at[4])
    small_copies = [
        pltpu.make_async_copy(source, target, local_sem.at[5 + n])
        for n, (source, target) in enumerate(
            (
                (tile_row_hbm, tile_row),
                (tile_col_hbm, tile_col),
                (tile_count_hbm, tile_count),
                (row_bits_hbm, row_bits),
                (col_bits_hbm, col_bits),
            )
        )
    ]
    for copy in small_copies + [u_copy, v_copy, x_copy, t_copy]:
        copy.start()

    barrier = pltpu.get_barrier_semaphore()
    pl.semaphore_signal(barrier, inc=1, device_id={"item": far_item}, device_id_type=MESH)
    pl.semaphore_signal(barrier, inc=1, device_id={"item": partner}, device_id_type=MESH)
    for d in range(1, chips):
        other = lax.rem(chip + d, chips) * 2 + core
        pl.semaphore_signal(barrier, inc=1, device_id={"item": other}, device_id_type=MESH)
    for d in range(1, n_user):
        pl.semaphore_signal(
            barrier, inc=1, device_id={"user": lax.rem(user + d, n_user)}, device_id_type=MESH
        )
    pl.semaphore_wait(barrier, 2 + (chips - 1) + (n_user - 1))

    panel_copies = []
    for which, (source, target) in enumerate(((item_hbm, v_all), (test_hbm, t_all))):
        for side, (window, device) in enumerate(((near_window, far_item), (far_window, partner))):
            panel_copies.append(
                pltpu.make_async_remote_copy(
                    src_ref=source,
                    dst_ref=target.at[window],
                    send_sem=panel_send_sem.at[which, side],
                    recv_sem=panel_recv_sem.at[which, side],
                    device_id={"item": device},
                    device_id_type=MESH,
                )
            )
            panel_copies[-1].start()

    for copy in small_copies:
        copy.wait()
    strip = 16
    lanes = lax.broadcasted_iota(jnp.int32, (strip, size), 1)
    rows = lax.broadcasted_iota(jnp.int32, (strip, size), 0)

    def make_mask(t, carry):
        live = (t < tile_count[0, 0]).astype(jnp.int32)
        words = jnp.zeros((strip, size), jnp.int32)
        for w in range(size // 32):
            words = jnp.where(lanes // 32 == w, col_bits[0, w, t] * live, words)
        col_seen = jnp.bitwise_and(lax.shift_right_logical(words, jnp.bitwise_and(lanes, 31)), 1)
        for s in range(size // strip):
            word = jnp.full((strip, size), row_bits[0, s * strip // 32, t], jnp.int32)
            seen = jnp.bitwise_and(
                lax.shift_right_logical(word, rows + (s * strip) % 32), col_seen
            )
            masks[t, s * strip : (s + 1) * strip, :] = seen.astype(F32).astype(BF16)
        return carry

    lax.fori_loop(0, slots, make_mask, 0)

    stride = 1 << (slots - 1).bit_length()
    order = []
    for t in range(slots):
        window = lax.rem(tile_col[0, t] - item + 1 + n_item, n_item)
        order.append((tile_row[0, t] * 3 + window) * stride + t)
    for a, b in sorting_pairs(slots):
        order[a], order[b] = jnp.minimum(order[a], order[b]), jnp.maximum(order[a], order[b])
    for t in range(slots):
        keys[t] = order[t]
    for group in range(blocks * 3 + 1):
        bounds[group] = sum((key < group * stride).astype(jnp.int32) for key in order)

    def predict(window):
        product = lax.dot_general(
            user_ref[...], v_all[window], (((1,), (1,)), ((), ())), preferred_element_type=F32
        )
        for r in range(blocks):
            p_buf[r * 3 + window] = product[r * size : (r + 1) * size]

    prefix[0] = jnp.zeros((size, size), F32)
    u_copy.wait()
    v_copy.wait()
    predict(1)
    panel_copies[1].wait_recv()
    predict(near_window)
    x_copy.wait()
    panel_copies[0].wait_recv()
    predict(far_window)

    def add_tile(i, carry):
        key = keys[i]
        t = jnp.bitwise_and(key, stride - 1)
        group = lax.shift_right_logical(key, stride.bit_length() - 1)
        for s in range(size // strip):
            at = slice(s * strip, (s + 1) * strip)
            gap = x_buf[t, at, :].astype(F32) - p_buf[group, at, :]
            residue = gap.astype(BF16) * masks[t, at, :]
            prefix[i + 1, at, :] = prefix[i, at, :] + residue.astype(F32)
        return carry

    lax.fori_loop(0, slots, add_tile, 0)

    def group_sum(r, window):
        group = r * 3 + window
        return prefix[bounds[group + 1]] - prefix[bounds[group]]

    def split_sums(r):
        for window in range(3):
            total = group_sum(r, window)
            high = total.astype(BF16)
            a_hi[r, window] = high
            a_lo[r, window] = (total - high.astype(F32)).astype(BF16)

    split_sums(1 - core)
    t_copy.wait()
    panel_copies[3].wait_recv()
    panel_copies[2].wait_recv()

    def sketch_block(r):
        total = None
        for window in range(3):
            for part in (a_hi, a_lo):
                term = jnp.dot(part[r, window], t_all[window], preferred_element_type=F32)
                total = term if total is None else total + term
        return total

    step = size // CHUNKS
    half_send[...] = sketch_block(1 - core)
    half_copies = []
    for j in range(CHUNKS):
        at = pl.ds(j * step, step)
        half_copies.append(
            pltpu.make_async_remote_copy(
                src_ref=half_send.at[at],
                dst_ref=half_recv.at[at],
                send_sem=half_send_sem.at[j],
                recv_sem=half_recv_sem.at[j],
                device_id={"item": partner},
                device_id_type=MESH,
            )
        )
        half_copies[-1].start()
    split_sums(core)
    own_half[...] = sketch_block(core)

    chip_copies = []
    for j in range(CHUNKS):
        at = pl.ds(j * step, step)
        half_copies[j].wait_recv()
        gathered[chip, at, :] = (own_half[at, :] + half_recv[at, :]).astype(BF16)
        for d in range(1, chips):
            chip_copies.append(
                pltpu.make_async_remote_copy(
                    src_ref=gathered.at[chip, at],
                    dst_ref=gathered.at[chip, at],
                    send_sem=chip_send_sem.at[j, d - 1],
                    recv_sem=chip_recv_sem.at[j, d - 1],
                    device_id={"item": lax.rem(chip + d, chips) * 2 + core},
                    device_id_type=MESH,
                )
            )
            chip_copies[-1].start()

    for r in range(blocks):
        for window in range(3):
            turned = group_sum(r, window).T
            high = turned.astype(BF16)
            at_hi[r, window] = high
            at_lo[r, window] = (turned - high.astype(F32)).astype(BF16)

    y_copies = []
    for j in range(CHUNKS):
        at = pl.ds(j * step, step)
        for d in range(1, chips):
            chip_copies[j * (chips - 1) + d - 1].wait_recv()
        total = gathered[0, at, :].astype(F32)
        for other in range(1, chips):
            total = total + gathered[other, at, :].astype(F32)
        y_full[core, at, :] = total
        y_copies.append(
            pltpu.make_async_remote_copy(
                src_ref=y_full.at[core, at],
                dst_ref=y_full.at[core, at],
                send_sem=y_send_sem.at[j],
                recv_sem=y_recv_sem.at[j],
                device_id={"item": partner},
                device_id_type=MESH,
            )
        )
        y_copies[-1].start()
    def second(r, window, y_half):
        return jnp.dot(at_hi[r, window], y_half, preferred_element_type=F32) + jnp.dot(
            at_lo[r, window], y_half, preferred_element_type=F32
        )

    y_half = y_full[core].astype(BF16)
    for window in range(3):
        z_part[window] = second(core, window, y_half)
    for j in range(CHUNKS):
        y_copies[j].wait_recv()
    out_copy = pltpu.make_async_copy(y_full, sketch_out, local_sem.at[3])
    out_copy.start()
    y_half = y_full[1 - core].astype(BF16)

    def term(window):
        return (z_part[window] + second(1 - core, window, y_half)).reshape(n_user, piece, size)

    piece = size // n_user
    turns = sorted(range(1, n_user), key=lambda d: -min(d, n_user - d)) + [0]
    z_copies = [[], []]
    for side, (window, device, z_send, z_recv) in enumerate(
        ((far_window, far_item, far_send, far_recv), (near_window, partner, near_send, near_recv))
    ):
        z_send[...] = term(window).astype(z_send.dtype)
        for n, d in enumerate(turns):
            target = lax.rem(user + d, n_user)
            z_copies[side].append(
                pltpu.make_async_remote_copy(
                    src_ref=z_send.at[target],
                    dst_ref=z_recv.at[target],
                    send_sem=z_send_sem.at[side, n],
                    recv_sem=z_recv_sem.at[side, n],
                    device_id={"item": device},
                    device_id_type=MESH,
                )
            )
            z_copies[side][-1].start()
    z_own[...] = term(1)

    piece_copies = []
    for n, d in enumerate(turns):
        target = lax.rem(user + d, n_user)
        z_copies[1][n].wait_recv()
        z_copies[0][n].wait_recv()
        total = z_own[target] + near_recv[target] + far_recv[target].astype(F32)
        if d == 0:
            piece_own[...] = total
            continue
        piece_send[target] = total.astype(piece_send.dtype)
        piece_copies.append(
            pltpu.make_async_remote_copy(
                src_ref=piece_send.at[target],
                dst_ref=piece_recv.at[n],
                send_sem=piece_send_sem.at[n],
                recv_sem=piece_recv_sem.at[n],
                device_id={"user": target},
                device_id_type=MESH,
            )
        )
        piece_copies[-1].start()
    total = piece_own[...]
    for n, copy in enumerate(piece_copies):
        copy.wait_recv()
        total = total + piece_recv[n].astype(F32)
    second_out[0] = total * scale

    out_copy.wait()
    for copy in panel_copies + half_copies + chip_copies + y_copies + z_copies[0] + z_copies[1]:
        copy.wait_send()
    for copy in piece_copies:
        copy.wait_send()


def hand_over(sketch, second, sketch_out, second_out, sketch_buf, second_buf, sem):
    triples = [(second, second_buf, second_out)]
    half = sketch.shape[1] // 2
    for r in range(sketch.shape[0]):
        for h in range(2):
            at = pl.ds(h * half, half)
            triples.append((sketch.at[r, at], sketch_buf.at[r, at], sketch_out.at[r, at]))
    reads, writes = [], []
    for n, (source, buffer, target) in enumerate(triples):
        reads.append(pltpu.make_async_copy(source, buffer, sem.at[0, n]))
        writes.append(pltpu.make_async_copy(buffer, target, sem.at[1, n]))
        reads[-1].start()
    for read, write in zip(reads, writes):
        read.wait()
        write.start()
    for write in writes:
        write.wait()


def shards(
    xtiles, row_bits, col_bits, tile_row, tile_col, tile_count, user_panel, item_panel, test_panel
):
    size = item_panel.shape[0]
    slots = xtiles.shape[1]
    blocks = user_panel.shape[0] // size
    n_user, n_item = lax.axis_size("user"), lax.axis_size("item")
    chips = n_item // 2
    piece = size // n_user
    sent = BF16 if piece % 16 == 0 else F32
    scale = 2.0 / math.sqrt(n_user * slots * size)
    square = (size, size)
    words = row_bits.shape[2]
    dma = pltpu.SemaphoreType.DMA
    vmem = pl.BlockSpec(memory_space=pltpu.VMEM)
    hbm = pl.BlockSpec(memory_space=pltpu.HBM)
    sketch, second = pl.pallas_call(
        functools.partial(kernel, n_user, n_item, scale),
        out_shape=(
            jax.ShapeDtypeStruct((blocks,) + square, F32),
            jax.ShapeDtypeStruct((1, piece, size), F32),
        ),
        in_specs=[hbm] * 9,
        out_specs=(hbm, vmem),
        scratch_shapes=[
            pltpu.SMEM((1, words, slots), jnp.int32),
            pltpu.SMEM((1, words, slots), jnp.int32),
            pltpu.SMEM((1, slots), jnp.int32),
            pltpu.SMEM((1, slots), jnp.int32),
            pltpu.SMEM((1, 1), jnp.int32),
            pltpu.VMEM(user_panel.shape, BF16),
            pltpu.VMEM((slots,) + square, BF16),
            pltpu.VMEM((slots,) + square, BF16),
            pltpu.VMEM((3,) + square, BF16),
            pltpu.VMEM((3,) + square, BF16),
            pltpu.VMEM((blocks * 3,) + square, F32),
            pltpu.VMEM((slots + 1,) + square, F32),
            pltpu.SMEM((slots,), jnp.int32),
            pltpu.SMEM((blocks * 3 + 1,), jnp.int32),
            pltpu.VMEM((blocks, 3) + square, BF16),
            pltpu.VMEM((blocks, 3) + square, BF16),
            pltpu.VMEM((blocks, 3) + square, BF16),
            pltpu.VMEM((blocks, 3) + square, BF16),
            pltpu.VMEM(square, F32),
            pltpu.VMEM(square, F32),
            pltpu.VMEM(square, F32),
            pltpu.VMEM((chips,) + square, BF16),
            pltpu.VMEM((blocks,) + square, F32),
            pltpu.VMEM((3,) + square, F32),
            pltpu.VMEM((n_user, piece, size), sent),
            pltpu.VMEM((n_user, piece, size), sent),
            pltpu.VMEM((n_user, piece, size), F32),
            pltpu.VMEM((n_user, piece, size), F32),
            pltpu.VMEM((n_user, piece, size), F32),
            pltpu.VMEM((piece, size), F32),
            pltpu.VMEM((n_user, piece, size), sent),
            pltpu.VMEM((n_user - 1, piece, size), sent),
            dma((10,)),
            dma((2, 2)),
            dma((2, 2)),
            dma((CHUNKS,)),
            dma((CHUNKS,)),
            dma((CHUNKS, chips - 1)),
            dma((CHUNKS, chips - 1)),
            dma((CHUNKS,)),
            dma((CHUNKS,)),
            dma((2, n_user)),
            dma((2, n_user)),
            dma((n_user - 1,)),
            dma((n_user - 1,)),
        ],
        compiler_params=pltpu.CompilerParams(
            collective_id=0, has_side_effects=True, vmem_limit_bytes=63 * 1024 * 1024
        ),
    )(
        jnp.swapaxes(row_bits, 1, 2),
        jnp.swapaxes(col_bits, 1, 2),
        tile_row,
        tile_col,
        tile_count,
        user_panel,
        xtiles,
        item_panel,
        test_panel,
    )
    sketch, second = pl.pallas_call(
        hand_over,
        out_shape=(
            jax.ShapeDtypeStruct(sketch.shape, F32),
            jax.ShapeDtypeStruct(second.shape, F32),
        ),
        in_specs=[hbm] * 2,
        out_specs=(hbm, hbm),
        scratch_shapes=[
            pltpu.VMEM(sketch.shape, F32),
            pltpu.VMEM(second.shape, F32),
            dma((2, 2 * blocks + 1)),
        ],
        compiler_params=pltpu.CompilerParams(vmem_limit_bytes=63 * 1024 * 1024),
    )(sketch, second)
    return sketch.reshape(blocks * size, size), second


def solution(mesh):
    placed = (
        P("user", "item", None, None),
        P("user", "item", None),
        P("user", "item", None),
        P("user", "item"),
        P("user", "item"),
        P("user", "item"),
        P("user", None),
        P("item", None),
        P("item", None),
    )
    return jax.shard_map(
        shards,
        mesh=mesh,
        in_specs=placed,
        out_specs=(P("user", None), P("item", "user", None)),
        check_vma=False,
    )
```

```python
import functools
import math

import jax
import jax.numpy as jnp
from jax import lax
from jax.experimental import pallas as pl
from jax.experimental.pallas import tpu as pltpu
from jax.sharding import PartitionSpec as P

MESH = pl.DeviceIdType.MESH
F32 = jnp.float32
BF16 = jnp.bfloat16
CHUNKS = 4


def sorting_pairs(length):
    size = 1 << (length - 1).bit_length()
    pairs = []
    p = 1
    while p < size:
        k = p
        while k >= 1:
            for j in range(k % p, size - k, 2 * k):
                for i in range(min(k, size - j - k)):
                    if (i + j) // (2 * p) == (i + j + k) // (2 * p):
                        pairs.append((i + j, i + j + k))
            k //= 2
        p *= 2
    return [(a, b) for a, b in pairs if b < length]


def kernel(
    n_user,
    n_item,
    scale,
    row_bits_hbm,
    col_bits_hbm,
    tile_row_hbm,
    tile_col_hbm,
    tile_count_hbm,
    user_hbm,
    x_hbm,
    item_hbm,
    test_hbm,
    sketch_out,
    second_out,
    row_bits,
    col_bits,
    tile_row,
    tile_col,
    tile_count,
    user_ref,
    x_buf,
    masks,
    v_all,
    t_all,
    p_buf,
    prefix,
    keys,
    bounds,
    a_hi,
    a_lo,
    at_hi,
    at_lo,
    half_send,
    half_recv,
    own_half,
    gathered,
    y_full,
    z_part,
    far_send,
    far_recv,
    near_send,
    near_recv,
    z_own,
    piece_own,
    piece_send,
    piece_recv,
    local_sem,
    panel_send_sem,
    panel_recv_sem,
    half_send_sem,
    half_recv_sem,
    chip_send_sem,
    chip_recv_sem,
    y_send_sem,
    y_recv_sem,
    z_send_sem,
    z_recv_sem,
    piece_send_sem,
    piece_recv_sem,
):
    user = lax.axis_index("user")
    item = lax.axis_index("item")
    core = lax.rem(item, 2)
    chip = item // 2
    chips = n_item // 2
    slots, size = x_buf.shape[0], x_buf.shape[1]
    blocks = user_ref.shape[0] // size
    lower = lax.rem(item + n_item - 1, n_item)
    upper = lax.rem(item + 1, n_item)
    partner = chip * 2 + 1 - core
    far_window = 2 * core
    near_window = 2 - far_window
    far_item = jnp.where(core == 0, lower, upper)

    x_copy = pltpu.make_async_copy(x_hbm.at[0], x_buf, local_sem.at[0])
    v_copy = pltpu.make_async_copy(item_hbm, v_all.at[1], local_sem.at[1])
    t_copy = pltpu.make_async_copy(test_hbm, t_all.at[1], local_sem.at[2])
    u_copy = pltpu.make_async_copy(user_hbm, user_ref, local_sem.at[4])
    small_copies = [
        pltpu.make_async_copy(source, target, local_sem.at[5 + n])
        for n, (source, target) in enumerate(
            (
                (tile_row_hbm, tile_row),
                (tile_col_hbm, tile_col),
                (tile_count_hbm, tile_count),
                (row_bits_hbm, row_bits),
                (col_bits_hbm, col_bits),
            )
        )
    ]
    for copy in small_copies + [u_copy, v_copy, x_copy, t_copy]:
        copy.start()

    barrier = pltpu.get_barrier_semaphore()
    pl.semaphore_signal(barrier, inc=1, device_id={"item": far_item}, device_id_type=MESH)
    pl.semaphore_signal(barrier, inc=1, device_id={"item": partner}, device_id_type=MESH)
    for d in range(1, chips):
        other = lax.rem(chip + d, chips) * 2 + core
        pl.semaphore_signal(barrier, inc=1, device_id={"item": other}, device_id_type=MESH)
    for d in range(1, n_user):
        pl.semaphore_signal(
            barrier, inc=1, device_id={"user": lax.rem(user + d, n_user)}, device_id_type=MESH
        )
    pl.semaphore_wait(barrier, 2 + (chips - 1) + (n_user - 1))

    half = size // 2
    panel_copies = [
        pltpu.make_async_remote_copy(
            src_ref=source.at[pl.ds(start, count)],
            dst_ref=target.at[window, pl.ds(start, count)],
            send_sem=panel_send_sem.at[n],
            recv_sem=panel_recv_sem.at[n],
            device_id={"item": device},
            device_id_type=MESH,
        )
        for n, (source, target, window, device, start, count) in enumerate(
            (
                (item_hbm, v_all, near_window, far_item, 0, half),
                (item_hbm, v_all, far_window, partner, 0, size),
                (item_hbm, v_all, near_window, far_item, half, half),
                (test_hbm, t_all, near_window, far_item, 0, size),
                (test_hbm, t_all, far_window, partner, 0, size),
            )
        )
    ]
    for copy in panel_copies:
        copy.start()

    for copy in small_copies:
        copy.wait()
    strip = 16
    lanes = lax.broadcasted_iota(jnp.int32, (strip, size), 1)
    rows = lax.broadcasted_iota(jnp.int32, (strip, size), 0)

    def make_mask(t, carry):
        live = (t < tile_count[0, 0]).astype(jnp.int32)
        words = jnp.zeros((strip, size), jnp.int32)
        for w in range(size // 32):
            words = jnp.where(lanes // 32 == w, col_bits[0, w, t] * live, words)
        col_seen = jnp.bitwise_and(lax.shift_right_logical(words, jnp.bitwise_and(lanes, 31)), 1)
        for s in range(size // strip):
            word = jnp.full((strip, size), row_bits[0, s * strip // 32, t], jnp.int32)
            seen = jnp.bitwise_and(
                lax.shift_right_logical(word, rows + (s * strip) % 32), col_seen
            )
            masks[t, s * strip : (s + 1) * strip, :] = seen.astype(F32).astype(BF16)
        return carry

    lax.fori_loop(0, slots, make_mask, 0, unroll=2)

    stride = 1 << (slots - 1).bit_length()
    order = []
    for t in range(slots):
        window = lax.rem(tile_col[0, t] - item + 1 + n_item, n_item)
        order.append((tile_row[0, t] * 3 + window) * stride + t)
    for a, b in sorting_pairs(slots):
        order[a], order[b] = jnp.minimum(order[a], order[b]), jnp.maximum(order[a], order[b])
    for t in range(slots):
        keys[t] = order[t]
    for group in range(blocks * 3 + 1):
        bounds[group] = sum((key < group * stride).astype(jnp.int32) for key in order)

    def predict(window, h):
        product = lax.dot_general(
            user_ref[...],
            v_all[window, h * half : (h + 1) * half],
            (((1,), (1,)), ((), ())),
            preferred_element_type=F32,
        )
        for r in range(blocks):
            p_buf[h, r * 3 + window] = product[r * size : (r + 1) * size]

    prefix[0] = jnp.zeros((size, size), F32)
    u_copy.wait()
    v_copy.wait()
    for h in range(2):
        predict(1, h)
    panel_copies[1].wait_recv()
    for h in range(2):
        predict(near_window, h)
    x_copy.wait()

    for h in range(2):
        panel_copies[2 * h].wait_recv()
        predict(far_window, h)
        columns = slice(h * half, (h + 1) * half)

        def add_tile(i, sums):
            key = keys[i]
            t = jnp.bitwise_and(key, stride - 1)
            group = lax.shift_right_logical(key, stride.bit_length() - 1)
            new = []
            for s, total in enumerate(sums):
                at = slice(s * strip, (s + 1) * strip)
                gap = x_buf[t, at, columns].astype(F32) - p_buf[h, group, at, :]
                residue = gap.astype(BF16) * masks[t, at, columns]
                new.append(total + residue.astype(F32))
                prefix[i + 1, at, columns] = new[-1]
            return tuple(new)

        zero = jnp.zeros((strip, half), F32)
        lax.fori_loop(0, slots, add_tile, (zero,) * (size // strip), unroll=4)

    def group_sum(r, window):
        group = r * 3 + window
        return prefix[bounds[group + 1]] - prefix[bounds[group]]

    def split_sums(r):
        for window in range(3):
            total = group_sum(r, window)
            high = total.astype(BF16)
            a_hi[r, window] = high
            a_lo[r, window] = (total - high.astype(F32)).astype(BF16)

    split_sums(1 - core)
    t_copy.wait()
    panel_copies[4].wait_recv()
    panel_copies[3].wait_recv()

    def sketch_block(r):
        total = None
        for window in range(3):
            for part in (a_hi, a_lo):
                term = jnp.dot(part[r, window], t_all[window], preferred_element_type=F32)
                total = term if total is None else total + term
        return total

    step = size // CHUNKS
    half_send[...] = sketch_block(1 - core)
    half_copies = []
    for j in range(CHUNKS):
        at = pl.ds(j * step, step)
        half_copies.append(
            pltpu.make_async_remote_copy(
                src_ref=half_send.at[at],
                dst_ref=half_recv.at[at],
                send_sem=half_send_sem.at[j],
                recv_sem=half_recv_sem.at[j],
                device_id={"item": partner},
                device_id_type=MESH,
            )
        )
        half_copies[-1].start()
    split_sums(core)
    own_half[...] = sketch_block(core)

    chip_copies = []
    for j in range(CHUNKS):
        at = pl.ds(j * step, step)
        half_copies[j].wait_recv()
        gathered[chip, at, :] = (own_half[at, :] + half_recv[at, :]).astype(BF16)
        for d in range(1, chips):
            chip_copies.append(
                pltpu.make_async_remote_copy(
                    src_ref=gathered.at[chip, at],
                    dst_ref=gathered.at[chip, at],
                    send_sem=chip_send_sem.at[j, d - 1],
                    recv_sem=chip_recv_sem.at[j, d - 1],
                    device_id={"item": lax.rem(chip + d, chips) * 2 + core},
                    device_id_type=MESH,
                )
            )
            chip_copies[-1].start()

    for r in range(blocks):
        for window in range(3):
            turned = group_sum(r, window).T
            high = turned.astype(BF16)
            at_hi[r, window] = high
            at_lo[r, window] = (turned - high.astype(F32)).astype(BF16)

    y_copies = []
    for j in range(CHUNKS):
        at = pl.ds(j * step, step)
        for d in range(1, chips):
            chip_copies[j * (chips - 1) + d - 1].wait_recv()
        total = gathered[0, at, :].astype(F32)
        for other in range(1, chips):
            total = total + gathered[other, at, :].astype(F32)
        y_full[core, at, :] = total
        y_copies.append(
            pltpu.make_async_remote_copy(
                src_ref=y_full.at[core, at],
                dst_ref=y_full.at[core, at],
                send_sem=y_send_sem.at[j],
                recv_sem=y_recv_sem.at[j],
                device_id={"item": partner},
                device_id_type=MESH,
            )
        )
        y_copies[-1].start()
    def second(r, window, y_half):
        return jnp.dot(at_hi[r, window], y_half, preferred_element_type=F32) + jnp.dot(
            at_lo[r, window], y_half, preferred_element_type=F32
        )

    y_half = y_full[core].astype(BF16)
    for window in range(3):
        z_part[window] = second(core, window, y_half)
    for j in range(CHUNKS):
        y_copies[j].wait_recv()
    out_copy = pltpu.make_async_copy(y_full, sketch_out, local_sem.at[3])
    out_copy.start()
    y_half = y_full[1 - core].astype(BF16)

    def term(window):
        return (z_part[window] + second(1 - core, window, y_half)).reshape(n_user, piece, size)

    piece = size // n_user
    turns = sorted(range(1, n_user), key=lambda d: -min(d, n_user - d)) + [0]
    z_copies = [[], []]
    for side, (window, device, z_send, z_recv) in enumerate(
        ((far_window, far_item, far_send, far_recv), (near_window, partner, near_send, near_recv))
    ):
        z_send[...] = term(window).astype(z_send.dtype)
        for n, d in enumerate(turns):
            target = lax.rem(user + d, n_user)
            z_copies[side].append(
                pltpu.make_async_remote_copy(
                    src_ref=z_send.at[target],
                    dst_ref=z_recv.at[target],
                    send_sem=z_send_sem.at[side, n],
                    recv_sem=z_recv_sem.at[side, n],
                    device_id={"item": device},
                    device_id_type=MESH,
                )
            )
            z_copies[side][-1].start()
    z_own[...] = term(1)

    piece_copies = []
    for n, d in enumerate(turns):
        target = lax.rem(user + d, n_user)
        z_copies[1][n].wait_recv()
        z_copies[0][n].wait_recv()
        total = z_own[target] + near_recv[target] + far_recv[target].astype(F32)
        if d == 0:
            piece_own[...] = total
            continue
        piece_send[target] = total.astype(piece_send.dtype)
        piece_copies.append(
            pltpu.make_async_remote_copy(
                src_ref=piece_send.at[target],
                dst_ref=piece_recv.at[n],
                send_sem=piece_send_sem.at[n],
                recv_sem=piece_recv_sem.at[n],
                device_id={"user": target},
                device_id_type=MESH,
            )
        )
        piece_copies[-1].start()
    total = piece_own[...]
    for n, copy in enumerate(piece_copies):
        copy.wait_recv()
        total = total + piece_recv[n].astype(F32)
    second_out[0] = total * scale

    out_copy.wait()
    for copy in panel_copies + half_copies + chip_copies + y_copies + z_copies[0] + z_copies[1]:
        copy.wait_send()
    for copy in piece_copies:
        copy.wait_send()


def hand_over(sketch, second, sketch_out, second_out, sem):
    copies = [
        pltpu.make_async_copy(second, second_out, sem.at[0]),
        pltpu.make_async_copy(sketch, sketch_out, sem.at[1]),
    ]
    for copy in copies:
        copy.start()
    for copy in copies:
        copy.wait()


def shards(
    xtiles, row_bits, col_bits, tile_row, tile_col, tile_count, user_panel, item_panel, test_panel
):
    size = item_panel.shape[0]
    slots = xtiles.shape[1]
    blocks = user_panel.shape[0] // size
    n_user, n_item = lax.axis_size("user"), lax.axis_size("item")
    chips = n_item // 2
    piece = size // n_user
    sent = BF16 if piece % 16 == 0 else F32
    scale = 2.0 / math.sqrt(n_user * slots * size)
    square = (size, size)
    words = row_bits.shape[2]
    dma = pltpu.SemaphoreType.DMA
    vmem = pl.BlockSpec(memory_space=pltpu.VMEM)
    hbm = pl.BlockSpec(memory_space=pltpu.HBM)
    sketch, second = pl.pallas_call(
        functools.partial(kernel, n_user, n_item, scale),
        out_shape=(
            pltpu.VMEM((blocks,) + square, F32),
            pltpu.VMEM((1, piece, size), F32),
        ),
        in_specs=[hbm] * 9,
        out_specs=(vmem, vmem),
        scratch_shapes=[
            pltpu.SMEM((1, words, slots), jnp.int32),
            pltpu.SMEM((1, words, slots), jnp.int32),
            pltpu.SMEM((1, slots), jnp.int32),
            pltpu.SMEM((1, slots), jnp.int32),
            pltpu.SMEM((1, 1), jnp.int32),
            pltpu.VMEM(user_panel.shape, BF16),
            pltpu.VMEM((slots,) + square, BF16),
            pltpu.VMEM((slots,) + square, BF16),
            pltpu.VMEM((3,) + square, BF16),
            pltpu.VMEM((3,) + square, BF16),
            pltpu.VMEM((2, blocks * 3, size, size // 2), F32),
            pltpu.VMEM((slots + 1,) + square, F32),
            pltpu.SMEM((slots,), jnp.int32),
            pltpu.SMEM((blocks * 3 + 1,), jnp.int32),
            pltpu.VMEM((blocks, 3) + square, BF16),
            pltpu.VMEM((blocks, 3) + square, BF16),
            pltpu.VMEM((blocks, 3) + square, BF16),
            pltpu.VMEM((blocks, 3) + square, BF16),
            pltpu.VMEM(square, F32),
            pltpu.VMEM(square, F32),
            pltpu.VMEM(square, F32),
            pltpu.VMEM((chips,) + square, BF16),
            pltpu.VMEM((blocks,) + square, F32),
            pltpu.VMEM((3,) + square, F32),
            pltpu.VMEM((n_user, piece, size), sent),
            pltpu.VMEM((n_user, piece, size), sent),
            pltpu.VMEM((n_user, piece, size), F32),
            pltpu.VMEM((n_user, piece, size), F32),
            pltpu.VMEM((n_user, piece, size), F32),
            pltpu.VMEM((piece, size), F32),
            pltpu.VMEM((n_user, piece, size), sent),
            pltpu.VMEM((n_user - 1, piece, size), sent),
            dma((10,)),
            dma((5,)),
            dma((5,)),
            dma((CHUNKS,)),
            dma((CHUNKS,)),
            dma((CHUNKS, chips - 1)),
            dma((CHUNKS, chips - 1)),
            dma((CHUNKS,)),
            dma((CHUNKS,)),
            dma((2, n_user)),
            dma((2, n_user)),
            dma((n_user - 1,)),
            dma((n_user - 1,)),
        ],
        compiler_params=pltpu.CompilerParams(
            collective_id=0, has_side_effects=True, vmem_limit_bytes=48 * 1024 * 1024
        ),
    )(
        *(
            operand
            if operand.size == 1
            else pltpu.with_memory_space_constraint(operand, pltpu.HBM)
            for operand in (
                jnp.swapaxes(row_bits, 1, 2),
                jnp.swapaxes(col_bits, 1, 2),
                tile_row,
                tile_col,
                tile_count,
                user_panel,
                xtiles,
                item_panel,
                test_panel,
            )
        )
    )
    sketch, second = pl.pallas_call(
        hand_over,
        out_shape=(
            jax.ShapeDtypeStruct(sketch.shape, F32),
            jax.ShapeDtypeStruct(second.shape, F32),
        ),
        in_specs=[vmem] * 2,
        out_specs=(hbm, hbm),
        scratch_shapes=[
            dma((2,)),
        ],
        compiler_params=pltpu.CompilerParams(vmem_limit_bytes=1024 * 1024),
    )(sketch, second)
    return sketch.reshape(blocks * size, size), second


def solution(mesh):
    placed = (
        P("user", "item", None, None),
        P("user", "item", None),
        P("user", "item", None),
        P("user", "item"),
        P("user", "item"),
        P("user", "item"),
        P("user", None),
        P("item", None),
        P("item", None),
    )
    return jax.shard_map(
        shards,
        mesh=mesh,
        in_specs=placed,
        out_specs=(P("user", None), P("item", "user", None)),
        check_vma=False,
    )
```

```python
import functools
import math

import jax
import jax.numpy as jnp
from jax import lax
from jax.experimental import pallas as pl
from jax.experimental.pallas import tpu as pltpu
from jax.sharding import PartitionSpec as P

MESH = pl.DeviceIdType.MESH
F32 = jnp.float32
BF16 = jnp.bfloat16
CHUNKS = 4


def sorting_pairs(length):
    size = 1 << (length - 1).bit_length()
    pairs = []
    p = 1
    while p < size:
        k = p
        while k >= 1:
            for j in range(k % p, size - k, 2 * k):
                for i in range(min(k, size - j - k)):
                    if (i + j) // (2 * p) == (i + j + k) // (2 * p):
                        pairs.append((i + j, i + j + k))
            k //= 2
        p *= 2
    return [(a, b) for a, b in pairs if b < length]


def wrapped(index, size):
    return jnp.where(index >= size, index - size, index)


def kernel(
    n_user,
    n_item,
    scale,
    row_bits_hbm,
    col_bits_hbm,
    tile_row_hbm,
    tile_col_hbm,
    tile_count_hbm,
    user_hbm,
    x_hbm,
    item_hbm,
    test_hbm,
    sketch_out,
    second_out,
    row_bits,
    col_bits,
    tile_row,
    tile_col,
    tile_count,
    user_ref,
    x_buf,
    row_masks,
    col_masks,
    v_all,
    t_all,
    p_buf,
    prefix,
    keys,
    bounds,
    a_hi,
    a_lo,
    at_hi,
    at_lo,
    half_send,
    half_recv,
    own_half,
    gathered,
    y_full,
    z_part,
    far_send,
    far_recv,
    near_send,
    near_recv,
    z_own,
    piece_own,
    piece_send,
    piece_recv,
    local_sem,
    panel_send_sem,
    panel_recv_sem,
    half_send_sem,
    half_recv_sem,
    chip_send_sem,
    chip_recv_sem,
    y_send_sem,
    y_recv_sem,
    z_send_sem,
    z_recv_sem,
    piece_send_sem,
    piece_recv_sem,
):
    user = lax.axis_index("user")
    item = lax.axis_index("item")
    core = lax.rem(item, 2)
    chip = item // 2
    chips = n_item // 2
    slots, size = x_buf.shape[0], x_buf.shape[1]
    blocks = user_ref.shape[0] // size
    lower = wrapped(item + n_item - 1, n_item)
    upper = wrapped(item + 1, n_item)
    partner = chip * 2 + 1 - core
    far_window = 2 * core
    near_window = 2 - far_window
    far_item = jnp.where(core == 0, lower, upper)

    x_copy = pltpu.make_async_copy(x_hbm.at[0], x_buf, local_sem.at[0])
    v_copy = pltpu.make_async_copy(item_hbm, v_all.at[1], local_sem.at[1])
    t_copy = pltpu.make_async_copy(test_hbm, t_all.at[1], local_sem.at[2])
    u_copy = pltpu.make_async_copy(user_hbm, user_ref, local_sem.at[4])
    small_copies = [
        pltpu.make_async_copy(source, target, local_sem.at[5 + n])
        for n, (source, target) in enumerate(
            (
                (tile_row_hbm, tile_row),
                (tile_col_hbm, tile_col),
                (tile_count_hbm, tile_count),
                (row_bits_hbm, row_bits),
                (col_bits_hbm, col_bits),
            )
        )
    ]
    for copy in small_copies + [u_copy, v_copy, x_copy, t_copy]:
        copy.start()

    barrier = pltpu.get_barrier_semaphore()
    pl.semaphore_signal(barrier, inc=1, device_id={"item": far_item}, device_id_type=MESH)
    pl.semaphore_signal(barrier, inc=1, device_id={"item": partner}, device_id_type=MESH)
    for d in range(1, chips):
        other = wrapped(chip + d, chips) * 2 + core
        pl.semaphore_signal(barrier, inc=1, device_id={"item": other}, device_id_type=MESH)
    for d in range(1, n_user):
        pl.semaphore_signal(
            barrier, inc=1, device_id={"user": wrapped(user + d, n_user)}, device_id_type=MESH
        )
    pl.semaphore_wait(barrier, 2 + (chips - 1) + (n_user - 1))

    half = size // 2
    panel_copies = [
        pltpu.make_async_remote_copy(
            src_ref=source.at[pl.ds(start, count)],
            dst_ref=target.at[window, pl.ds(start, count)],
            send_sem=panel_send_sem.at[n],
            recv_sem=panel_recv_sem.at[n],
            device_id={"item": device},
            device_id_type=MESH,
        )
        for n, (source, target, window, device, start, count) in enumerate(
            (
                (item_hbm, v_all, near_window, far_item, 0, half),
                (item_hbm, v_all, far_window, partner, 0, size),
                (item_hbm, v_all, near_window, far_item, half, half),
                (test_hbm, t_all, near_window, far_item, 0, size),
                (test_hbm, t_all, far_window, partner, 0, size),
            )
        )
    ]
    for copy in panel_copies:
        copy.start()

    for copy in small_copies:
        copy.wait()
    strip = 16
    lanes = lax.broadcasted_iota(jnp.int32, (strip, size), 1)
    rows = lax.broadcasted_iota(jnp.int32, (strip, half), 0)

    def make_mask(t, carry):
        live = (t < tile_count[0, 0]).astype(jnp.int32)
        words = jnp.zeros((strip, size), jnp.int32)
        for w in range(size // 32):
            words = jnp.where(lanes // 32 == w, col_bits[0, w, t] * live, words)
        seen = jnp.bitwise_and(lax.shift_right_logical(words, jnp.bitwise_and(lanes, 31)), 1)
        col_masks[t] = seen.astype(F32).astype(BF16)
        for s in range(size // strip):
            word = jnp.full((strip, half), row_bits[0, s * strip // 32, t], jnp.int32)
            seen = jnp.bitwise_and(lax.shift_right_logical(word, rows + (s * strip) % 32), 1)
            row_masks[t, s * strip : (s + 1) * strip, :] = seen.astype(F32).astype(BF16)
        return carry

    lax.fori_loop(0, slots, make_mask, 0, unroll=4)

    stride = 1 << (slots - 1).bit_length()
    order = []
    for t in range(slots):
        window = wrapped(wrapped(tile_col[0, t] - item + 1 + n_item, n_item), n_item)
        order.append((tile_row[0, t] * 3 + window) * stride + t)
    for a, b in sorting_pairs(slots):
        order[a], order[b] = jnp.minimum(order[a], order[b]), jnp.maximum(order[a], order[b])
    for t in range(slots):
        keys[t] = order[t]
    for group in range(blocks * 3 + 1):
        bounds[group] = sum((key < group * stride).astype(jnp.int32) for key in order)

    def predict(window, h):
        product = lax.dot_general(
            user_ref[...],
            v_all[window, h * half : (h + 1) * half],
            (((1,), (1,)), ((), ())),
            preferred_element_type=F32,
        )
        for r in range(blocks):
            p_buf[h, r * 3 + window] = product[r * size : (r + 1) * size]

    prefix[0] = jnp.zeros((size, size), F32)
    u_copy.wait()
    v_copy.wait()
    for h in range(2):
        predict(1, h)
    panel_copies[1].wait_recv()
    for h in range(2):
        predict(near_window, h)
    x_copy.wait()

    for h in range(2):
        panel_copies[2 * h].wait_recv()
        predict(far_window, h)
        columns = slice(h * half, (h + 1) * half)

        def add_tile(i, sums):
            key = keys[i]
            t = jnp.bitwise_and(key, stride - 1)
            group = lax.shift_right_logical(key, stride.bit_length() - 1)
            col_mask = col_masks[t, :, columns]
            new = []
            for s, total in enumerate(sums):
                at = slice(s * strip, (s + 1) * strip)
                gap = x_buf[t, at, columns].astype(F32) - p_buf[h, group, at, :]
                residue = gap.astype(BF16) * (row_masks[t, at, :] * col_mask)
                new.append(total + residue.astype(F32))
                prefix[i + 1, at, columns] = new[-1]
            return tuple(new)

        zero = jnp.zeros((strip, half), F32)
        lax.fori_loop(0, slots, add_tile, (zero,) * (size // strip), unroll=4)

    def group_sum(r, window):
        group = r * 3 + window
        return prefix[bounds[group + 1]] - prefix[bounds[group]]

    def split_sums(r):
        for window in range(3):
            total = group_sum(r, window)
            high = total.astype(BF16)
            a_hi[r, window] = high
            a_lo[r, window] = (total - high.astype(F32)).astype(BF16)

    split_sums(1 - core)
    t_copy.wait()
    panel_copies[4].wait_recv()
    panel_copies[3].wait_recv()

    def sketch_block(r):
        total = None
        for window in range(3):
            for part in (a_hi, a_lo):
                term = jnp.dot(part[r, window], t_all[window], preferred_element_type=F32)
                total = term if total is None else total + term
        return total

    step = size // CHUNKS
    half_send[...] = sketch_block(1 - core)
    half_copies = []
    for j in range(CHUNKS):
        at = pl.ds(j * step, step)
        half_copies.append(
            pltpu.make_async_remote_copy(
                src_ref=half_send.at[at],
                dst_ref=half_recv.at[at],
                send_sem=half_send_sem.at[j],
                recv_sem=half_recv_sem.at[j],
                device_id={"item": partner},
                device_id_type=MESH,
            )
        )
        half_copies[-1].start()
    split_sums(core)
    own_half[...] = sketch_block(core)

    chip_copies = []
    for j in range(CHUNKS):
        at = pl.ds(j * step, step)
        half_copies[j].wait_recv()
        gathered[chip, at, :] = (own_half[at, :] + half_recv[at, :]).astype(BF16)
        for d in range(1, chips):
            chip_copies.append(
                pltpu.make_async_remote_copy(
                    src_ref=gathered.at[chip, at],
                    dst_ref=gathered.at[chip, at],
                    send_sem=chip_send_sem.at[j, d - 1],
                    recv_sem=chip_recv_sem.at[j, d - 1],
                    device_id={"item": wrapped(chip + d, chips) * 2 + core},
                    device_id_type=MESH,
                )
            )
            chip_copies[-1].start()

    for r in range(blocks):
        for window in range(3):
            turned = group_sum(r, window).T
            high = turned.astype(BF16)
            at_hi[r, window] = high
            at_lo[r, window] = (turned - high.astype(F32)).astype(BF16)

    y_copies = []
    for j in range(CHUNKS):
        at = pl.ds(j * step, step)
        for d in range(1, chips):
            chip_copies[j * (chips - 1) + d - 1].wait_recv()
        total = gathered[0, at, :].astype(F32)
        for other in range(1, chips):
            total = total + gathered[other, at, :].astype(F32)
        y_full[core, at, :] = total
        y_copies.append(
            pltpu.make_async_remote_copy(
                src_ref=y_full.at[core, at],
                dst_ref=y_full.at[core, at],
                send_sem=y_send_sem.at[j],
                recv_sem=y_recv_sem.at[j],
                device_id={"item": partner},
                device_id_type=MESH,
            )
        )
        y_copies[-1].start()
    def second(r, window, y_half):
        return jnp.dot(at_hi[r, window], y_half, preferred_element_type=F32) + jnp.dot(
            at_lo[r, window], y_half, preferred_element_type=F32
        )

    y_half = y_full[core].astype(BF16)
    for window in range(3):
        z_part[window] = second(core, window, y_half)
    for j in range(CHUNKS):
        y_copies[j].wait_recv()
    out_copy = pltpu.make_async_copy(y_full, sketch_out, local_sem.at[3])
    out_copy.start()
    y_half = y_full[1 - core].astype(BF16)

    def term(window):
        return (z_part[window] + second(1 - core, window, y_half)).reshape(n_user, piece, size)

    piece = size // n_user
    turns = sorted(range(1, n_user), key=lambda d: -min(d, n_user - d)) + [0]
    z_copies = [[], []]
    for side, (window, device, z_send, z_recv) in enumerate(
        ((far_window, far_item, far_send, far_recv), (near_window, partner, near_send, near_recv))
    ):
        z_send[...] = term(window).astype(z_send.dtype)
        for n, d in enumerate(turns):
            target = wrapped(user + d, n_user)
            z_copies[side].append(
                pltpu.make_async_remote_copy(
                    src_ref=z_send.at[target],
                    dst_ref=z_recv.at[target],
                    send_sem=z_send_sem.at[side, n],
                    recv_sem=z_recv_sem.at[side, n],
                    device_id={"item": device},
                    device_id_type=MESH,
                )
            )
            z_copies[side][-1].start()
    z_own[...] = term(1)

    piece_copies = []
    for n, d in enumerate(turns):
        target = wrapped(user + d, n_user)
        z_copies[1][n].wait_recv()
        z_copies[0][n].wait_recv()
        total = z_own[target] + near_recv[target] + far_recv[target].astype(F32)
        if d == 0:
            piece_own[...] = total
            continue
        piece_send[target] = total.astype(piece_send.dtype)
        piece_copies.append(
            pltpu.make_async_remote_copy(
                src_ref=piece_send.at[target],
                dst_ref=piece_recv.at[n],
                send_sem=piece_send_sem.at[n],
                recv_sem=piece_recv_sem.at[n],
                device_id={"user": target},
                device_id_type=MESH,
            )
        )
        piece_copies[-1].start()
    total = piece_own[...]
    for n, copy in enumerate(piece_copies):
        copy.wait_recv()
        total = total + piece_recv[n].astype(F32)
    second_out[0] = total * scale

    out_copy.wait()
    for copy in panel_copies + half_copies + chip_copies + y_copies + z_copies[0] + z_copies[1]:
        copy.wait_send()
    for copy in piece_copies:
        copy.wait_send()


def hand_over(sketch, second, sketch_out, second_out, sem):
    copies = [
        pltpu.make_async_copy(second, second_out, sem.at[0]),
        pltpu.make_async_copy(sketch, sketch_out, sem.at[1]),
    ]
    for copy in copies:
        copy.start()
    for copy in copies:
        copy.wait()


def shards(
    xtiles, row_bits, col_bits, tile_row, tile_col, tile_count, user_panel, item_panel, test_panel
):
    size = item_panel.shape[0]
    slots = xtiles.shape[1]
    blocks = user_panel.shape[0] // size
    n_user, n_item = lax.axis_size("user"), lax.axis_size("item")
    chips = n_item // 2
    piece = size // n_user
    sent = BF16 if piece % 16 == 0 else F32
    scale = 2.0 / math.sqrt(n_user * slots * size)
    square = (size, size)
    words = row_bits.shape[2]
    dma = pltpu.SemaphoreType.DMA
    vmem = pl.BlockSpec(memory_space=pltpu.VMEM)
    hbm = pl.BlockSpec(memory_space=pltpu.HBM)
    sketch, second = pl.pallas_call(
        functools.partial(kernel, n_user, n_item, scale),
        out_shape=(
            pltpu.VMEM((blocks,) + square, F32),
            pltpu.VMEM((1, piece, size), F32),
        ),
        in_specs=[hbm] * 9,
        out_specs=(vmem, vmem),
        scratch_shapes=[
            pltpu.SMEM((1, words, slots), jnp.int32),
            pltpu.SMEM((1, words, slots), jnp.int32),
            pltpu.SMEM((1, slots), jnp.int32),
            pltpu.SMEM((1, slots), jnp.int32),
            pltpu.SMEM((1, 1), jnp.int32),
            pltpu.VMEM(user_panel.shape, BF16),
            pltpu.VMEM((slots,) + square, BF16),
            pltpu.VMEM((slots, size, size // 2), BF16),
            pltpu.VMEM((slots, 16, size), BF16),
            pltpu.VMEM((3,) + square, BF16),
            pltpu.VMEM((3,) + square, BF16),
            pltpu.VMEM((2, blocks * 3, size, size // 2), F32),
            pltpu.VMEM((slots + 1,) + square, F32),
            pltpu.SMEM((slots,), jnp.int32),
            pltpu.SMEM((blocks * 3 + 1,), jnp.int32),
            pltpu.VMEM((blocks, 3) + square, BF16),
            pltpu.VMEM((blocks, 3) + square, BF16),
            pltpu.VMEM((blocks, 3) + square, BF16),
            pltpu.VMEM((blocks, 3) + square, BF16),
            pltpu.VMEM(square, F32),
            pltpu.VMEM(square, F32),
            pltpu.VMEM(square, F32),
            pltpu.VMEM((chips,) + square, BF16),
            pltpu.VMEM((blocks,) + square, F32),
            pltpu.VMEM((3,) + square, F32),
            pltpu.VMEM((n_user, piece, size), sent),
            pltpu.VMEM((n_user, piece, size), sent),
            pltpu.VMEM((n_user, piece, size), F32),
            pltpu.VMEM((n_user, piece, size), F32),
            pltpu.VMEM((n_user, piece, size), F32),
            pltpu.VMEM((piece, size), F32),
            pltpu.VMEM((n_user, piece, size), sent),
            pltpu.VMEM((n_user - 1, piece, size), sent),
            dma((10,)),
            dma((5,)),
            dma((5,)),
            dma((CHUNKS,)),
            dma((CHUNKS,)),
            dma((CHUNKS, chips - 1)),
            dma((CHUNKS, chips - 1)),
            dma((CHUNKS,)),
            dma((CHUNKS,)),
            dma((2, n_user)),
            dma((2, n_user)),
            dma((n_user - 1,)),
            dma((n_user - 1,)),
        ],
        compiler_params=pltpu.CompilerParams(
            collective_id=0, has_side_effects=True, vmem_limit_bytes=48 * 1024 * 1024
        ),
    )(
        *(
            operand
            if operand.size == 1
            else pltpu.with_memory_space_constraint(operand, pltpu.HBM)
            for operand in (
                jnp.swapaxes(row_bits, 1, 2),
                jnp.swapaxes(col_bits, 1, 2),
                tile_row,
                tile_col,
                tile_count,
                user_panel,
                xtiles,
                item_panel,
                test_panel,
            )
        )
    )
    sketch, second = pl.pallas_call(
        hand_over,
        out_shape=(
            jax.ShapeDtypeStruct(sketch.shape, F32),
            jax.ShapeDtypeStruct(second.shape, F32),
        ),
        in_specs=[vmem] * 2,
        out_specs=(hbm, hbm),
        scratch_shapes=[
            dma((2,)),
        ],
        compiler_params=pltpu.CompilerParams(vmem_limit_bytes=1024 * 1024),
    )(sketch, second)
    return sketch.reshape(blocks * size, size), second


def solution(mesh):
    placed = (
        P("user", "item", None, None),
        P("user", "item", None),
        P("user", "item", None),
        P("user", "item"),
        P("user", "item"),
        P("user", "item"),
        P("user", None),
        P("item", None),
        P("item", None),
    )
    return jax.shard_map(
        shards,
        mesh=mesh,
        in_specs=placed,
        out_specs=(P("user", None), P("item", "user", None)),
        check_vma=False,
    )
```

```python
import functools
import math

import jax
import jax.numpy as jnp
from jax import lax
from jax.experimental import pallas as pl
from jax.experimental.pallas import tpu as pltpu
from jax.sharding import PartitionSpec as P

MESH = pl.DeviceIdType.MESH
F32 = jnp.float32
BF16 = jnp.bfloat16
CHUNKS = 4


def sorting_pairs(length):
    size = 1 << (length - 1).bit_length()
    pairs = []
    p = 1
    while p < size:
        k = p
        while k >= 1:
            for j in range(k % p, size - k, 2 * k):
                for i in range(min(k, size - j - k)):
                    if (i + j) // (2 * p) == (i + j + k) // (2 * p):
                        pairs.append((i + j, i + j + k))
            k //= 2
        p *= 2
    return [(a, b) for a, b in pairs if b < length]


def wrapped(index, size):
    return jnp.where(index >= size, index - size, index)


def kernel(
    n_user,
    n_item,
    scale,
    row_bits_hbm,
    col_bits_hbm,
    tile_row_hbm,
    tile_col_hbm,
    tile_count_hbm,
    user_hbm,
    x_hbm,
    item_hbm,
    test_hbm,
    sketch_out,
    second_out,
    row_bits,
    col_bits,
    tile_row,
    tile_col,
    tile_count,
    user_ref,
    x_buf,
    row_masks,
    col_masks,
    v_all,
    t_all,
    p_buf,
    prefix,
    keys,
    bounds,
    a_hi,
    a_lo,
    at_hi,
    at_lo,
    half_send,
    half_recv,
    own_half,
    gathered,
    y_full,
    z_part,
    far_send,
    far_recv,
    near_send,
    near_recv,
    z_own,
    piece_own,
    piece_send,
    piece_recv,
    local_sem,
    panel_send_sem,
    panel_recv_sem,
    half_send_sem,
    half_recv_sem,
    chip_send_sem,
    chip_recv_sem,
    y_send_sem,
    y_recv_sem,
    z_send_sem,
    z_recv_sem,
    piece_send_sem,
    piece_recv_sem,
):
    user = lax.axis_index("user")
    item = lax.axis_index("item")
    core = lax.rem(item, 2)
    chip = item // 2
    chips = n_item // 2
    slots, size = x_buf.shape[0], x_buf.shape[1]
    blocks = user_ref.shape[0] // size
    lower = wrapped(item + n_item - 1, n_item)
    upper = wrapped(item + 1, n_item)
    partner = chip * 2 + 1 - core
    far_window = 2 * core
    near_window = 2 - far_window
    far_item = jnp.where(core == 0, lower, upper)

    x_copy = pltpu.make_async_copy(x_hbm.at[0], x_buf, local_sem.at[0])
    v_copy = pltpu.make_async_copy(item_hbm, v_all.at[1], local_sem.at[1])
    t_copy = pltpu.make_async_copy(test_hbm, t_all.at[1], local_sem.at[2])
    u_copy = pltpu.make_async_copy(user_hbm, user_ref, local_sem.at[4])
    small_copies = [
        pltpu.make_async_copy(source, target, local_sem.at[5 + n])
        for n, (source, target) in enumerate(
            (
                (tile_row_hbm, tile_row),
                (tile_col_hbm, tile_col),
                (tile_count_hbm, tile_count),
                (row_bits_hbm, row_bits),
                (col_bits_hbm, col_bits),
            )
        )
    ]
    for copy in small_copies + [u_copy, v_copy, x_copy, t_copy]:
        copy.start()

    barrier = pltpu.get_barrier_semaphore()
    pl.semaphore_signal(barrier, inc=1, device_id={"item": far_item}, device_id_type=MESH)
    pl.semaphore_signal(barrier, inc=1, device_id={"item": partner}, device_id_type=MESH)
    for d in range(1, chips):
        other = wrapped(chip + d, chips) * 2 + core
        pl.semaphore_signal(barrier, inc=1, device_id={"item": other}, device_id_type=MESH)
    for d in range(1, n_user):
        pl.semaphore_signal(
            barrier, inc=1, device_id={"user": wrapped(user + d, n_user)}, device_id_type=MESH
        )
    pl.semaphore_wait(barrier, 2 + (chips - 1) + (n_user - 1))

    half = size // 2
    parity = lax.rem(user, 2)
    buddy = user + 1 - 2 * parity
    halves = [pl.ds(pl.multiple_of(h * half, half), half) for h in (parity, 1 - parity)]
    panel_copies = []

    def panel_copy(source, target, device):
        n = len(panel_copies)
        panel_copies.append(
            pltpu.make_async_remote_copy(
                src_ref=source,
                dst_ref=target,
                send_sem=panel_send_sem.at[n],
                recv_sem=panel_recv_sem.at[n],
                device_id=device,
                device_id_type=MESH,
            )
        )
        panel_copies[-1].start()
        return panel_copies[-1]

    far_device, near_device = {"item": far_item}, {"item": partner}
    far_v = panel_copy(item_hbm.at[halves[0]], v_all.at[near_window, halves[0]], far_device)
    near_v = panel_copy(item_hbm, v_all.at[far_window], near_device)
    far_t = panel_copy(test_hbm.at[halves[0]], t_all.at[near_window, halves[0]], far_device)
    near_t = panel_copy(test_hbm, t_all.at[far_window], near_device)

    def swap(panels):
        block = panels.at[far_window, halves[0]]
        return panel_copy(block, block, {"user": buddy})

    for copy in small_copies:
        copy.wait()
    strip = 16
    lanes = lax.broadcasted_iota(jnp.int32, (strip, size), 1)
    rows = lax.broadcasted_iota(jnp.int32, (strip, half), 0)

    def make_mask(t, carry):
        live = (t < tile_count[0, 0]).astype(jnp.int32)
        words = jnp.zeros((strip, size), jnp.int32)
        for w in range(size // 32):
            words = jnp.where(lanes // 32 == w, col_bits[0, w, t] * live, words)
        seen = jnp.bitwise_and(lax.shift_right_logical(words, jnp.bitwise_and(lanes, 31)), 1)
        col_masks[t] = seen.astype(F32).astype(BF16)
        for s in range(size // strip):
            word = jnp.full((strip, half), row_bits[0, s * strip // 32, t], jnp.int32)
            seen = jnp.bitwise_and(lax.shift_right_logical(word, rows + (s * strip) % 32), 1)
            row_masks[t, s * strip : (s + 1) * strip, :] = seen.astype(F32).astype(BF16)
        return carry

    lax.fori_loop(0, slots, make_mask, 0, unroll=4)

    stride = 1 << (slots - 1).bit_length()
    order = []
    for t in range(slots):
        window = wrapped(wrapped(tile_col[0, t] - item + 1 + n_item, n_item), n_item)
        order.append((tile_row[0, t] * 3 + window) * stride + t)
    for a, b in sorting_pairs(slots):
        order[a], order[b] = jnp.minimum(order[a], order[b]), jnp.maximum(order[a], order[b])
    for t in range(slots):
        keys[t] = order[t]
    for group in range(blocks * 3 + 1):
        bounds[group] = sum((key < group * stride).astype(jnp.int32) for key in order)

    def predict(window, h):
        product = lax.dot_general(
            user_ref[...],
            v_all[window, halves[h]],
            (((1,), (1,)), ((), ())),
            preferred_element_type=F32,
        )
        for r in range(blocks):
            p_buf[h, r * 3 + window] = product[r * size : (r + 1) * size]

    prefix[0] = jnp.zeros((size, size), F32)
    u_copy.wait()
    v_copy.wait()
    for h in range(2):
        predict(1, h)
    near_v.wait_recv()
    for h in range(2):
        predict(near_window, h)
    far_v.wait_recv()
    swapped_v = swap(v_all)
    x_copy.wait()

    for h in range(2):
        if h == 1:
            far_t.wait_recv()
            swapped_t = swap(t_all)
            swapped_v.wait_recv()
        predict(far_window, h)
        columns = halves[h]

        def add_tile(i, sums):
            key = keys[i]
            t = jnp.bitwise_and(key, stride - 1)
            group = lax.shift_right_logical(key, stride.bit_length() - 1)
            col_mask = col_masks[t, :, columns]
            new = []
            for s, total in enumerate(sums):
                at = slice(s * strip, (s + 1) * strip)
                gap = x_buf[t, at, columns].astype(F32) - p_buf[h, group, at, :]
                residue = gap.astype(BF16) * (row_masks[t, at, :] * col_mask)
                new.append(total + residue.astype(F32))
                prefix[i + 1, at, columns] = new[-1]
            return tuple(new)

        zero = jnp.zeros((strip, half), F32)
        lax.fori_loop(0, slots, add_tile, (zero,) * (size // strip), unroll=4)

    def group_sum(r, window):
        group = r * 3 + window
        return prefix[bounds[group + 1]] - prefix[bounds[group]]

    def split_sums(r):
        for window in range(3):
            total = group_sum(r, window)
            high = total.astype(BF16)
            a_hi[r, window] = high
            a_lo[r, window] = (total - high.astype(F32)).astype(BF16)

    split_sums(1 - core)
    t_copy.wait()
    near_t.wait_recv()
    swapped_t.wait_recv()

    def sketch_block(r):
        total = None
        for window in range(3):
            for part in (a_hi, a_lo):
                term = jnp.dot(part[r, window], t_all[window], preferred_element_type=F32)
                total = term if total is None else total + term
        return total

    step = size // CHUNKS
    half_send[...] = sketch_block(1 - core)
    half_copies = []
    for j in range(CHUNKS):
        at = pl.ds(j * step, step)
        half_copies.append(
            pltpu.make_async_remote_copy(
                src_ref=half_send.at[at],
                dst_ref=half_recv.at[at],
                send_sem=half_send_sem.at[j],
                recv_sem=half_recv_sem.at[j],
                device_id={"item": partner},
                device_id_type=MESH,
            )
        )
        half_copies[-1].start()
    split_sums(core)
    own_half[...] = sketch_block(core)

    chip_copies = []
    for j in range(CHUNKS):
        at = pl.ds(j * step, step)
        half_copies[j].wait_recv()
        gathered[chip, at, :] = (own_half[at, :] + half_recv[at, :]).astype(BF16)
        for d in range(1, chips):
            chip_copies.append(
                pltpu.make_async_remote_copy(
                    src_ref=gathered.at[chip, at],
                    dst_ref=gathered.at[chip, at],
                    send_sem=chip_send_sem.at[j, d - 1],
                    recv_sem=chip_recv_sem.at[j, d - 1],
                    device_id={"item": wrapped(chip + d, chips) * 2 + core},
                    device_id_type=MESH,
                )
            )
            chip_copies[-1].start()

    for r in range(blocks):
        for window in range(3):
            turned = group_sum(r, window).T
            high = turned.astype(BF16)
            at_hi[r, window] = high
            at_lo[r, window] = (turned - high.astype(F32)).astype(BF16)

    y_copies = []
    for j in range(CHUNKS):
        at = pl.ds(j * step, step)
        for d in range(1, chips):
            chip_copies[j * (chips - 1) + d - 1].wait_recv()
        total = gathered[0, at, :].astype(F32)
        for other in range(1, chips):
            total = total + gathered[other, at, :].astype(F32)
        y_full[core, at, :] = total
        y_copies.append(
            pltpu.make_async_remote_copy(
                src_ref=y_full.at[core, at],
                dst_ref=y_full.at[core, at],
                send_sem=y_send_sem.at[j],
                recv_sem=y_recv_sem.at[j],
                device_id={"item": partner},
                device_id_type=MESH,
            )
        )
        y_copies[-1].start()
    def second(r, window, y_half):
        return jnp.dot(at_hi[r, window], y_half, preferred_element_type=F32) + jnp.dot(
            at_lo[r, window], y_half, preferred_element_type=F32
        )

    y_half = y_full[core].astype(BF16)
    for window in range(3):
        z_part[window] = second(core, window, y_half)
    for j in range(CHUNKS):
        y_copies[j].wait_recv()
    out_copy = pltpu.make_async_copy(y_full, sketch_out, local_sem.at[3])
    out_copy.start()
    y_half = y_full[1 - core].astype(BF16)

    def term(window):
        return (z_part[window] + second(1 - core, window, y_half)).reshape(n_user, piece, size)

    piece = size // n_user
    turns = sorted(range(1, n_user), key=lambda d: -min(d, n_user - d)) + [0]
    z_copies = [[], []]
    for side, (window, device, z_send, z_recv) in enumerate(
        ((far_window, far_item, far_send, far_recv), (near_window, partner, near_send, near_recv))
    ):
        z_send[...] = term(window).astype(z_send.dtype)
        for n, d in enumerate(turns):
            target = wrapped(user + d, n_user)
            z_copies[side].append(
                pltpu.make_async_remote_copy(
                    src_ref=z_send.at[target],
                    dst_ref=z_recv.at[target],
                    send_sem=z_send_sem.at[side, n],
                    recv_sem=z_recv_sem.at[side, n],
                    device_id={"item": device},
                    device_id_type=MESH,
                )
            )
            z_copies[side][-1].start()
    z_own[...] = term(1)

    piece_copies = []
    for n, d in enumerate(turns):
        target = wrapped(user + d, n_user)
        z_copies[1][n].wait_recv()
        z_copies[0][n].wait_recv()
        total = z_own[target] + near_recv[target] + far_recv[target].astype(F32)
        if d == 0:
            piece_own[...] = total
            continue
        piece_send[target] = total.astype(piece_send.dtype)
        piece_copies.append(
            pltpu.make_async_remote_copy(
                src_ref=piece_send.at[target],
                dst_ref=piece_recv.at[n],
                send_sem=piece_send_sem.at[n],
                recv_sem=piece_recv_sem.at[n],
                device_id={"user": target},
                device_id_type=MESH,
            )
        )
        piece_copies[-1].start()
    total = piece_own[...]
    for n, copy in enumerate(piece_copies):
        copy.wait_recv()
        total = total + piece_recv[n].astype(F32)
    second_out[0] = total * scale

    out_copy.wait()
    for copy in panel_copies + half_copies + chip_copies + y_copies + z_copies[0] + z_copies[1]:
        copy.wait_send()
    for copy in piece_copies:
        copy.wait_send()


def hand_over(sketch, second, sketch_out, second_out, sem):
    copies = [
        pltpu.make_async_copy(second, second_out, sem.at[0]),
        pltpu.make_async_copy(sketch, sketch_out, sem.at[1]),
    ]
    for copy in copies:
        copy.start()
    for copy in copies:
        copy.wait()


def shards(
    xtiles, row_bits, col_bits, tile_row, tile_col, tile_count, user_panel, item_panel, test_panel
):
    size = item_panel.shape[0]
    slots = xtiles.shape[1]
    blocks = user_panel.shape[0] // size
    n_user, n_item = lax.axis_size("user"), lax.axis_size("item")
    chips = n_item // 2
    piece = size // n_user
    sent = BF16 if piece % 16 == 0 else F32
    scale = 2.0 / math.sqrt(n_user * slots * size)
    square = (size, size)
    words = row_bits.shape[2]
    dma = pltpu.SemaphoreType.DMA
    vmem = pl.BlockSpec(memory_space=pltpu.VMEM)
    hbm = pl.BlockSpec(memory_space=pltpu.HBM)
    sketch, second = pl.pallas_call(
        functools.partial(kernel, n_user, n_item, scale),
        out_shape=(
            pltpu.VMEM((blocks,) + square, F32),
            pltpu.VMEM((1, piece, size), F32),
        ),
        in_specs=[hbm] * 9,
        out_specs=(vmem, vmem),
        scratch_shapes=[
            pltpu.SMEM((1, words, slots), jnp.int32),
            pltpu.SMEM((1, words, slots), jnp.int32),
            pltpu.SMEM((1, slots), jnp.int32),
            pltpu.SMEM((1, slots), jnp.int32),
            pltpu.SMEM((1, 1), jnp.int32),
            pltpu.VMEM(user_panel.shape, BF16),
            pltpu.VMEM((slots,) + square, BF16),
            pltpu.VMEM((slots, size, size // 2), BF16),
            pltpu.VMEM((slots, 16, size), BF16),
            pltpu.VMEM((3,) + square, BF16),
            pltpu.VMEM((3,) + square, BF16),
            pltpu.VMEM((2, blocks * 3, size, size // 2), F32),
            pltpu.VMEM((slots + 1,) + square, F32),
            pltpu.SMEM((slots,), jnp.int32),
            pltpu.SMEM((blocks * 3 + 1,), jnp.int32),
            pltpu.VMEM((blocks, 3) + square, BF16),
            pltpu.VMEM((blocks, 3) + square, BF16),
            pltpu.VMEM((blocks, 3) + square, BF16),
            pltpu.VMEM((blocks, 3) + square, BF16),
            pltpu.VMEM(square, F32),
            pltpu.VMEM(square, F32),
            pltpu.VMEM(square, F32),
            pltpu.VMEM((chips,) + square, BF16),
            pltpu.VMEM((blocks,) + square, F32),
            pltpu.VMEM((3,) + square, F32),
            pltpu.VMEM((n_user, piece, size), sent),
            pltpu.VMEM((n_user, piece, size), sent),
            pltpu.VMEM((n_user, piece, size), F32),
            pltpu.VMEM((n_user, piece, size), F32),
            pltpu.VMEM((n_user, piece, size), F32),
            pltpu.VMEM((piece, size), F32),
            pltpu.VMEM((n_user, piece, size), sent),
            pltpu.VMEM((n_user - 1, piece, size), sent),
            dma((10,)),
            dma((6,)),
            dma((6,)),
            dma((CHUNKS,)),
            dma((CHUNKS,)),
            dma((CHUNKS, chips - 1)),
            dma((CHUNKS, chips - 1)),
            dma((CHUNKS,)),
            dma((CHUNKS,)),
            dma((2, n_user)),
            dma((2, n_user)),
            dma((n_user - 1,)),
            dma((n_user - 1,)),
        ],
        compiler_params=pltpu.CompilerParams(
            collective_id=0, has_side_effects=True, vmem_limit_bytes=48 * 1024 * 1024
        ),
    )(
        *(
            operand
            if operand.size == 1
            else pltpu.with_memory_space_constraint(operand, pltpu.HBM)
            for operand in (
                jnp.swapaxes(row_bits, 1, 2),
                jnp.swapaxes(col_bits, 1, 2),
                tile_row,
                tile_col,
                tile_count,
                user_panel,
                xtiles,
                item_panel,
                test_panel,
            )
        )
    )
    sketch, second = pl.pallas_call(
        hand_over,
        out_shape=(
            jax.ShapeDtypeStruct(sketch.shape, F32),
            jax.ShapeDtypeStruct(second.shape, F32),
        ),
        in_specs=[vmem] * 2,
        out_specs=(hbm, hbm),
        scratch_shapes=[
            dma((2,)),
        ],
        compiler_params=pltpu.CompilerParams(vmem_limit_bytes=1024 * 1024),
    )(sketch, second)
    return sketch.reshape(blocks * size, size), second


def solution(mesh):
    placed = (
        P("user", "item", None, None),
        P("user", "item", None),
        P("user", "item", None),
        P("user", "item"),
        P("user", "item"),
        P("user", "item"),
        P("user", None),
        P("item", None),
        P("item", None),
    )
    return jax.shard_map(
        shards,
        mesh=mesh,
        in_specs=placed,
        out_specs=(P("user", None), P("item", "user", None)),
        check_vma=False,
    )
```

```python
import functools
import math

import jax
import jax.numpy as jnp
from jax import lax
from jax.experimental import pallas as pl
from jax.experimental.pallas import tpu as pltpu
from jax.sharding import PartitionSpec as P

MESH = pl.DeviceIdType.MESH
F32 = jnp.float32
BF16 = jnp.bfloat16
CHUNKS = 4


def sorting_pairs(length):
    size = 1 << (length - 1).bit_length()
    pairs = []
    p = 1
    while p < size:
        k = p
        while k >= 1:
            for j in range(k % p, size - k, 2 * k):
                for i in range(min(k, size - j - k)):
                    if (i + j) // (2 * p) == (i + j + k) // (2 * p):
                        pairs.append((i + j, i + j + k))
            k //= 2
        p *= 2
    return [(a, b) for a, b in pairs if b < length]


def wrapped(index, size):
    return jnp.where(index >= size, index - size, index)


def kernel(
    n_user,
    n_item,
    scale,
    row_bits_hbm,
    col_bits_hbm,
    tile_row_hbm,
    tile_col_hbm,
    tile_count_hbm,
    user_hbm,
    x_hbm,
    item_hbm,
    test_hbm,
    sketch_out,
    second_out,
    row_bits,
    col_bits,
    tile_row,
    tile_col,
    tile_count,
    user_ref,
    x_buf,
    row_masks,
    col_masks,
    v_all,
    t_all,
    p_buf,
    prefix,
    keys,
    bounds,
    a_hi,
    a_lo,
    at_both,
    s_part,
    half_send,
    half_recv,
    own_half,
    gathered,
    y_full,
    z_part,
    far_send,
    far_recv,
    near_send,
    near_recv,
    z_own,
    piece_own,
    piece_send,
    piece_recv,
    local_sem,
    panel_send_sem,
    panel_recv_sem,
    half_send_sem,
    half_recv_sem,
    chip_send_sem,
    chip_recv_sem,
    y_send_sem,
    y_recv_sem,
    z_send_sem,
    z_recv_sem,
    piece_send_sem,
    piece_recv_sem,
):
    user = lax.axis_index("user")
    item = lax.axis_index("item")
    core = lax.rem(item, 2)
    chip = item // 2
    chips = n_item // 2
    slots, size = x_buf.shape[0], x_buf.shape[1]
    blocks = user_ref.shape[0] // size
    lower = wrapped(item + n_item - 1, n_item)
    upper = wrapped(item + 1, n_item)
    partner = chip * 2 + 1 - core
    far_window = 2 * core
    near_window = 2 - far_window
    far_item = jnp.where(core == 0, lower, upper)

    x_copy = pltpu.make_async_copy(x_hbm.at[0], x_buf, local_sem.at[0])
    v_copy = pltpu.make_async_copy(item_hbm, v_all.at[1], local_sem.at[1])
    t_copy = pltpu.make_async_copy(test_hbm, t_all.at[1], local_sem.at[2])
    u_copy = pltpu.make_async_copy(user_hbm, user_ref, local_sem.at[4])
    small_copies = [
        pltpu.make_async_copy(source, target, local_sem.at[5 + n])
        for n, (source, target) in enumerate(
            (
                (tile_row_hbm, tile_row),
                (tile_col_hbm, tile_col),
                (tile_count_hbm, tile_count),
                (row_bits_hbm, row_bits),
                (col_bits_hbm, col_bits),
            )
        )
    ]
    for copy in small_copies + [u_copy, v_copy, x_copy, t_copy]:
        copy.start()

    barrier = pltpu.get_barrier_semaphore()
    pl.semaphore_signal(barrier, inc=1, device_id={"item": far_item}, device_id_type=MESH)
    pl.semaphore_signal(barrier, inc=1, device_id={"item": partner}, device_id_type=MESH)
    for d in range(1, chips):
        other = wrapped(chip + d, chips) * 2 + core
        pl.semaphore_signal(barrier, inc=1, device_id={"item": other}, device_id_type=MESH)
    for d in range(1, n_user):
        pl.semaphore_signal(
            barrier, inc=1, device_id={"user": wrapped(user + d, n_user)}, device_id_type=MESH
        )
    pl.semaphore_wait(barrier, 2 + (chips - 1) + (n_user - 1))

    half = size // 2
    panel_copies = [
        pltpu.make_async_remote_copy(
            src_ref=source.at[pl.ds(start, count)],
            dst_ref=target.at[window, pl.ds(start, count)],
            send_sem=panel_send_sem.at[n],
            recv_sem=panel_recv_sem.at[n],
            device_id={"item": device},
            device_id_type=MESH,
        )
        for n, (source, target, window, device, start, count) in enumerate(
            (
                (item_hbm, v_all, near_window, far_item, 0, half),
                (item_hbm, v_all, far_window, partner, 0, size),
                (item_hbm, v_all, near_window, far_item, half, half),
                (test_hbm, t_all, near_window, far_item, 0, size),
                (test_hbm, t_all, far_window, partner, 0, size),
            )
        )
    ]
    for copy in panel_copies:
        copy.start()

    for copy in small_copies:
        copy.wait()
    strip = 16
    lanes = lax.broadcasted_iota(jnp.int32, (strip, size), 1)
    rows = lax.broadcasted_iota(jnp.int32, (strip, half), 0)

    def make_mask(t, carry):
        live = (t < tile_count[0, 0]).astype(jnp.int32)
        words = jnp.zeros((strip, size), jnp.int32)
        for w in range(size // 32):
            words = jnp.where(lanes // 32 == w, col_bits[0, w, t] * live, words)
        seen = jnp.bitwise_and(lax.shift_right_logical(words, jnp.bitwise_and(lanes, 31)), 1)
        col_masks[t] = seen.astype(F32).astype(BF16)
        for s in range(size // strip):
            word = jnp.full((strip, half), row_bits[0, s * strip // 32, t], jnp.int32)
            seen = jnp.bitwise_and(lax.shift_right_logical(word, rows + (s * strip) % 32), 1)
            row_masks[t, s * strip : (s + 1) * strip, :] = seen.astype(F32).astype(BF16)
        return carry

    lax.fori_loop(0, slots, make_mask, 0, unroll=4)

    stride = 1 << (slots - 1).bit_length()
    order = []
    for t in range(slots):
        window = wrapped(wrapped(tile_col[0, t] - item + 1 + n_item, n_item), n_item)
        order.append((tile_row[0, t] * 3 + window) * stride + t)
    for a, b in sorting_pairs(slots):
        order[a], order[b] = jnp.minimum(order[a], order[b]), jnp.maximum(order[a], order[b])
    for t in range(slots):
        keys[t] = order[t]
    for group in range(blocks * 3 + 1):
        bounds[group] = sum((key < group * stride).astype(jnp.int32) for key in order)

    def predict(window, h):
        product = lax.dot_general(
            user_ref[...],
            v_all[window, h * half : (h + 1) * half],
            (((1,), (1,)), ((), ())),
            preferred_element_type=F32,
        )
        for r in range(blocks):
            p_buf[h, r * 3 + window] = product[r * size : (r + 1) * size]

    prefix[0] = jnp.zeros((size, size), F32)
    u_copy.wait()
    v_copy.wait()
    for h in range(2):
        predict(1, h)
    panel_copies[1].wait_recv()
    for h in range(2):
        predict(near_window, h)
    x_copy.wait()

    for h in range(2):
        panel_copies[2 * h].wait_recv()
        predict(far_window, h)
        columns = slice(h * half, (h + 1) * half)

        def add_tile(i, sums):
            key = keys[i]
            t = jnp.bitwise_and(key, stride - 1)
            group = lax.shift_right_logical(key, stride.bit_length() - 1)
            col_mask = col_masks[t, :, columns]
            new = []
            for s, total in enumerate(sums):
                at = slice(s * strip, (s + 1) * strip)
                gap = x_buf[t, at, columns].astype(F32) - p_buf[h, group, at, :]
                residue = gap.astype(BF16) * (row_masks[t, at, :] * col_mask)
                new.append(total + residue.astype(F32))
                prefix[i + 1, at, columns] = new[-1]
            return tuple(new)

        zero = jnp.zeros((strip, half), F32)
        lax.fori_loop(0, slots, add_tile, (zero,) * (size // strip), unroll=4)

    def group_sum(r, window):
        group = r * 3 + window
        return prefix[bounds[group + 1]] - prefix[bounds[group]]

    for r in (1 - core, core):
        for window in range(3):
            total = group_sum(r, window)
            high = total.astype(BF16)
            columns = slice(window * size, (window + 1) * size)
            a_hi[r, :, columns] = high
            a_lo[r, :, columns] = (total - high.astype(F32)).astype(BF16)

    def products(r, columns, panel):
        return jnp.dot(a_hi[r, :, columns], panel, preferred_element_type=F32) + jnp.dot(
            a_lo[r, :, columns], panel, preferred_element_type=F32
        )

    t_copy.wait()
    panel_copies[4].wait_recv()
    first = near_window // 2
    pair = pl.ds(pl.multiple_of(first * size, size), 2 * size)
    panel = t_all[pl.ds(first, 2)].reshape(2 * size, size)
    for r in (1 - core, core):
        s_part[r] = products(r, pair, panel)
    panel_copies[3].wait_recv()

    def sketch_block(r):
        far = pl.ds(pl.multiple_of(far_window * size, size), size)
        return s_part[r] + products(r, far, t_all[far_window])

    step = size // CHUNKS
    half_send[...] = sketch_block(1 - core)
    half_copies = []
    for j in range(CHUNKS):
        at = pl.ds(j * step, step)
        half_copies.append(
            pltpu.make_async_remote_copy(
                src_ref=half_send.at[at],
                dst_ref=half_recv.at[at],
                send_sem=half_send_sem.at[j],
                recv_sem=half_recv_sem.at[j],
                device_id={"item": partner},
                device_id_type=MESH,
            )
        )
        half_copies[-1].start()
    own_half[...] = sketch_block(core)

    chip_copies = []
    for j in range(CHUNKS):
        at = pl.ds(j * step, step)
        half_copies[j].wait_recv()
        gathered[chip, at, :] = (own_half[at, :] + half_recv[at, :]).astype(BF16)
        for d in range(1, chips):
            chip_copies.append(
                pltpu.make_async_remote_copy(
                    src_ref=gathered.at[chip, at],
                    dst_ref=gathered.at[chip, at],
                    send_sem=chip_send_sem.at[j, d - 1],
                    recv_sem=chip_recv_sem.at[j, d - 1],
                    device_id={"item": wrapped(chip + d, chips) * 2 + core},
                    device_id_type=MESH,
                )
            )
            chip_copies[-1].start()

    for r in range(blocks):
        for window in range(3):
            turned = group_sum(r, window).T
            high = turned.astype(BF16)
            at_both[r, window, :, :size] = high
            at_both[r, window, :, size:] = (turned - high.astype(F32)).astype(BF16)

    y_copies = []
    for j in range(CHUNKS):
        at = pl.ds(j * step, step)
        for d in range(1, chips):
            chip_copies[j * (chips - 1) + d - 1].wait_recv()
        total = gathered[0, at, :].astype(F32)
        for other in range(1, chips):
            total = total + gathered[other, at, :].astype(F32)
        y_full[core, at, :] = total
        y_copies.append(
            pltpu.make_async_remote_copy(
                src_ref=y_full.at[core, at],
                dst_ref=y_full.at[core, at],
                send_sem=y_send_sem.at[j],
                recv_sem=y_recv_sem.at[j],
                device_id={"item": partner},
                device_id_type=MESH,
            )
        )
        y_copies[-1].start()
    def second(r, window, y_half):
        return jnp.dot(
            at_both[r, window],
            jnp.concatenate([y_half, y_half], axis=0),
            preferred_element_type=F32,
        )

    y_half = y_full[core].astype(BF16)
    for window in range(3):
        z_part[window] = second(core, window, y_half)
    for j in range(CHUNKS):
        y_copies[j].wait_recv()
    out_copy = pltpu.make_async_copy(y_full, sketch_out, local_sem.at[3])
    out_copy.start()
    y_half = y_full[1 - core].astype(BF16)

    def term(window):
        return (z_part[window] + second(1 - core, window, y_half)).reshape(n_user, piece, size)

    piece = size // n_user
    turns = sorted(range(1, n_user), key=lambda d: -min(d, n_user - d)) + [0]
    far_send[...] = term(far_window).astype(far_send.dtype)
    z_copies = []
    for n, d in enumerate(turns):
        target = wrapped(user + d, n_user)
        z_copies.append(
            pltpu.make_async_remote_copy(
                src_ref=far_send.at[target],
                dst_ref=far_recv.at[target],
                send_sem=z_send_sem.at[n],
                recv_sem=z_recv_sem.at[n],
                device_id={"item": far_item},
                device_id_type=MESH,
            )
        )
        z_copies[-1].start()
    near_send[...] = term(near_window)
    near_copy = pltpu.make_async_remote_copy(
        src_ref=near_send,
        dst_ref=near_recv,
        send_sem=z_send_sem.at[n_user],
        recv_sem=z_recv_sem.at[n_user],
        device_id={"item": partner},
        device_id_type=MESH,
    )
    near_copy.start()
    z_own[...] = term(1)

    near_copy.wait_recv()
    z_own[...] = z_own[...] + near_recv[...]
    piece_copies = []
    for n, d in enumerate(turns):
        target = wrapped(user + d, n_user)
        z_copies[n].wait_recv()
        total = z_own[target] + far_recv[target].astype(F32)
        if d == 0:
            piece_own[...] = total
            continue
        piece_send[target] = total.astype(piece_send.dtype)
        piece_copies.append(
            pltpu.make_async_remote_copy(
                src_ref=piece_send.at[target],
                dst_ref=piece_recv.at[n],
                send_sem=piece_send_sem.at[n],
                recv_sem=piece_recv_sem.at[n],
                device_id={"user": target},
                device_id_type=MESH,
            )
        )
        piece_copies[-1].start()
    total = piece_own[...]
    for n, copy in enumerate(piece_copies):
        copy.wait_recv()
        total = total + piece_recv[n].astype(F32)
    second_out[0] = total * scale

    out_copy.wait()
    for copy in panel_copies + half_copies + chip_copies + y_copies + z_copies + [near_copy]:
        copy.wait_send()
    for copy in piece_copies:
        copy.wait_send()


def hand_over(sketch, second, sketch_out, second_out, sem):
    copies = [
        pltpu.make_async_copy(second, second_out, sem.at[0]),
        pltpu.make_async_copy(sketch, sketch_out, sem.at[1]),
    ]
    for copy in copies:
        copy.start()
    for copy in copies:
        copy.wait()


def shards(
    xtiles, row_bits, col_bits, tile_row, tile_col, tile_count, user_panel, item_panel, test_panel
):
    size = item_panel.shape[0]
    slots = xtiles.shape[1]
    blocks = user_panel.shape[0] // size
    n_user, n_item = lax.axis_size("user"), lax.axis_size("item")
    chips = n_item // 2
    piece = size // n_user
    sent = BF16 if piece % 16 == 0 else F32
    scale = 2.0 / math.sqrt(n_user * slots * size)
    square = (size, size)
    words = row_bits.shape[2]
    dma = pltpu.SemaphoreType.DMA
    vmem = pl.BlockSpec(memory_space=pltpu.VMEM)
    hbm = pl.BlockSpec(memory_space=pltpu.HBM)
    sketch, second = pl.pallas_call(
        functools.partial(kernel, n_user, n_item, scale),
        out_shape=(
            pltpu.VMEM((blocks,) + square, F32),
            pltpu.VMEM((1, piece, size), F32),
        ),
        in_specs=[hbm] * 9,
        out_specs=(vmem, vmem),
        scratch_shapes=[
            pltpu.SMEM((1, words, slots), jnp.int32),
            pltpu.SMEM((1, words, slots), jnp.int32),
            pltpu.SMEM((1, slots), jnp.int32),
            pltpu.SMEM((1, slots), jnp.int32),
            pltpu.SMEM((1, 1), jnp.int32),
            pltpu.VMEM(user_panel.shape, BF16),
            pltpu.VMEM((slots,) + square, BF16),
            pltpu.VMEM((slots, size, size // 2), BF16),
            pltpu.VMEM((slots, 16, size), BF16),
            pltpu.VMEM((3,) + square, BF16),
            pltpu.VMEM((3,) + square, BF16),
            pltpu.VMEM((2, blocks * 3, size, size // 2), F32),
            pltpu.VMEM((slots + 1,) + square, F32),
            pltpu.SMEM((slots,), jnp.int32),
            pltpu.SMEM((blocks * 3 + 1,), jnp.int32),
            pltpu.VMEM((blocks, size, 3 * size), BF16),
            pltpu.VMEM((blocks, size, 3 * size), BF16),
            pltpu.VMEM((blocks, 3, size, 2 * size), BF16),
            pltpu.VMEM((blocks,) + square, F32),
            pltpu.VMEM(square, F32),
            pltpu.VMEM(square, F32),
            pltpu.VMEM(square, F32),
            pltpu.VMEM((chips,) + square, BF16),
            pltpu.VMEM((blocks,) + square, F32),
            pltpu.VMEM((3,) + square, F32),
            pltpu.VMEM((n_user, piece, size), sent),
            pltpu.VMEM((n_user, piece, size), sent),
            pltpu.VMEM((n_user, piece, size), F32),
            pltpu.VMEM((n_user, piece, size), F32),
            pltpu.VMEM((n_user, piece, size), F32),
            pltpu.VMEM((piece, size), F32),
            pltpu.VMEM((n_user, piece, size), sent),
            pltpu.VMEM((n_user - 1, piece, size), sent),
            dma((10,)),
            dma((5,)),
            dma((5,)),
            dma((CHUNKS,)),
            dma((CHUNKS,)),
            dma((CHUNKS, chips - 1)),
            dma((CHUNKS, chips - 1)),
            dma((CHUNKS,)),
            dma((CHUNKS,)),
            dma((n_user + 1,)),
            dma((n_user + 1,)),
            dma((n_user - 1,)),
            dma((n_user - 1,)),
        ],
        compiler_params=pltpu.CompilerParams(
            collective_id=0, has_side_effects=True, vmem_limit_bytes=48 * 1024 * 1024
        ),
    )(
        *(
            operand
            if operand.size == 1
            else pltpu.with_memory_space_constraint(operand, pltpu.HBM)
            for operand in (
                jnp.swapaxes(row_bits, 1, 2),
                jnp.swapaxes(col_bits, 1, 2),
                tile_row,
                tile_col,
                tile_count,
                user_panel,
                xtiles,
                item_panel,
                test_panel,
            )
        )
    )
    sketch, second = pl.pallas_call(
        hand_over,
        out_shape=(
            jax.ShapeDtypeStruct(sketch.shape, F32),
            jax.ShapeDtypeStruct(second.shape, F32),
        ),
        in_specs=[vmem] * 2,
        out_specs=(hbm, hbm),
        scratch_shapes=[
            dma((2,)),
        ],
        compiler_params=pltpu.CompilerParams(vmem_limit_bytes=1024 * 1024),
    )(sketch, second)
    return sketch.reshape(blocks * size, size), second


def solution(mesh):
    placed = (
        P("user", "item", None, None),
        P("user", "item", None),
        P("user", "item", None),
        P("user", "item"),
        P("user", "item"),
        P("user", "item"),
        P("user", None),
        P("item", None),
        P("item", None),
    )
    return jax.shard_map(
        shards,
        mesh=mesh,
        in_specs=placed,
        out_specs=(P("user", None), P("item", "user", None)),
        check_vma=False,
    )
```

```python
import functools
import math

import jax
import jax.numpy as jnp
from jax import lax
from jax.experimental import pallas as pl
from jax.experimental.pallas import tpu as pltpu
from jax.sharding import PartitionSpec as P

MESH = pl.DeviceIdType.MESH
F32 = jnp.float32
BF16 = jnp.bfloat16
CHUNKS = 4


def sorting_pairs(length):
    size = 1 << (length - 1).bit_length()
    pairs = []
    p = 1
    while p < size:
        k = p
        while k >= 1:
            for j in range(k % p, size - k, 2 * k):
                for i in range(min(k, size - j - k)):
                    if (i + j) // (2 * p) == (i + j + k) // (2 * p):
                        pairs.append((i + j, i + j + k))
            k //= 2
        p *= 2
    return [(a, b) for a, b in pairs if b < length]


def wrapped(index, size):
    return jnp.where(index >= size, index - size, index)


def kernel(
    n_user,
    n_item,
    scale,
    row_bits_hbm,
    col_bits_hbm,
    tile_row_hbm,
    tile_col_hbm,
    tile_count_hbm,
    user_hbm,
    x_hbm,
    item_hbm,
    test_hbm,
    sketch_out,
    second_out,
    row_bits,
    col_bits,
    tile_row,
    tile_col,
    tile_count,
    user_ref,
    x_buf,
    row_masks,
    col_masks,
    v_all,
    t_all,
    p_buf,
    prefix,
    keys,
    bounds,
    a_hi,
    a_lo,
    at_both,
    s_part,
    half_send,
    half_recv,
    own_half,
    gathered,
    y_full,
    z_part,
    far_send,
    far_recv,
    near_send,
    near_recv,
    z_own,
    piece_own,
    piece_send,
    piece_recv,
    local_sem,
    panel_send_sem,
    panel_recv_sem,
    half_send_sem,
    half_recv_sem,
    chip_send_sem,
    chip_recv_sem,
    pair_send_sem,
    pair_recv_sem,
    z_send_sem,
    z_recv_sem,
    piece_send_sem,
    piece_recv_sem,
):
    user = lax.axis_index("user")
    item = lax.axis_index("item")
    core = lax.rem(item, 2)
    chip = item // 2
    chips = n_item // 2
    slots, size = x_buf.shape[0], x_buf.shape[1]
    blocks = user_ref.shape[0] // size
    lower = wrapped(item + n_item - 1, n_item)
    upper = wrapped(item + 1, n_item)
    partner = chip * 2 + 1 - core
    far_window = 2 * core
    near_window = 2 - far_window
    far_item = jnp.where(core == 0, lower, upper)

    x_copy = pltpu.make_async_copy(x_hbm.at[0], x_buf, local_sem.at[0])
    v_copy = pltpu.make_async_copy(item_hbm, v_all.at[1], local_sem.at[1])
    t_copy = pltpu.make_async_copy(test_hbm, t_all.at[1], local_sem.at[2])
    u_copy = pltpu.make_async_copy(user_hbm, user_ref, local_sem.at[4])
    small_copies = [
        pltpu.make_async_copy(source, target, local_sem.at[5 + n])
        for n, (source, target) in enumerate(
            (
                (tile_row_hbm, tile_row),
                (tile_col_hbm, tile_col),
                (tile_count_hbm, tile_count),
                (row_bits_hbm, row_bits),
                (col_bits_hbm, col_bits),
            )
        )
    ]
    for copy in small_copies + [u_copy, v_copy, x_copy, t_copy]:
        copy.start()

    barrier = pltpu.get_barrier_semaphore()
    pl.semaphore_signal(barrier, inc=1, device_id={"item": far_item}, device_id_type=MESH)
    pl.semaphore_signal(barrier, inc=1, device_id={"item": partner}, device_id_type=MESH)
    for d in range(1, chips):
        other = wrapped(chip + d, chips) * 2 + core
        pl.semaphore_signal(barrier, inc=1, device_id={"item": other}, device_id_type=MESH)
    for d in range(1, n_user):
        pl.semaphore_signal(
            barrier, inc=1, device_id={"user": wrapped(user + d, n_user)}, device_id_type=MESH
        )
    pl.semaphore_wait(barrier, 2 + (chips - 1) + (n_user - 1))

    half = size // 2
    panel_copies = [
        pltpu.make_async_remote_copy(
            src_ref=source.at[pl.ds(start, count)],
            dst_ref=target.at[window, pl.ds(start, count)],
            send_sem=panel_send_sem.at[n],
            recv_sem=panel_recv_sem.at[n],
            device_id={"item": device},
            device_id_type=MESH,
        )
        for n, (source, target, window, device, start, count) in enumerate(
            (
                (item_hbm, v_all, near_window, far_item, 0, half),
                (item_hbm, v_all, far_window, partner, 0, size),
                (item_hbm, v_all, near_window, far_item, half, half),
                (test_hbm, t_all, near_window, far_item, 0, size),
                (test_hbm, t_all, far_window, partner, 0, size),
            )
        )
    ]
    for copy in panel_copies:
        copy.start()

    for copy in small_copies:
        copy.wait()
    strip = 16
    lanes = lax.broadcasted_iota(jnp.int32, (strip, size), 1)
    rows = lax.broadcasted_iota(jnp.int32, (strip, half), 0)

    def make_mask(t, carry):
        live = (t < tile_count[0, 0]).astype(jnp.int32)
        words = jnp.zeros((strip, size), jnp.int32)
        for w in range(size // 32):
            words = jnp.where(lanes // 32 == w, col_bits[0, w, t] * live, words)
        seen = jnp.bitwise_and(lax.shift_right_logical(words, jnp.bitwise_and(lanes, 31)), 1)
        col_masks[t] = seen.astype(F32).astype(BF16)
        for s in range(size // strip):
            word = jnp.full((strip, half), row_bits[0, s * strip // 32, t], jnp.int32)
            seen = jnp.bitwise_and(lax.shift_right_logical(word, rows + (s * strip) % 32), 1)
            row_masks[t, s * strip : (s + 1) * strip, :] = seen.astype(F32).astype(BF16)
        return carry

    lax.fori_loop(0, slots, make_mask, 0, unroll=4)

    stride = 1 << (slots - 1).bit_length()
    order = []
    for t in range(slots):
        window = wrapped(wrapped(tile_col[0, t] - item + 1 + n_item, n_item), n_item)
        order.append((tile_row[0, t] * 3 + window) * stride + t)
    for a, b in sorting_pairs(slots):
        order[a], order[b] = jnp.minimum(order[a], order[b]), jnp.maximum(order[a], order[b])
    for t in range(slots):
        keys[t] = order[t]
    for group in range(blocks * 3 + 1):
        bounds[group] = sum((key < group * stride).astype(jnp.int32) for key in order)

    def predict(window, h):
        product = lax.dot_general(
            user_ref[...],
            v_all[window, h * half : (h + 1) * half],
            (((1,), (1,)), ((), ())),
            preferred_element_type=F32,
        )
        for r in range(blocks):
            p_buf[h, r * 3 + window] = product[r * size : (r + 1) * size]

    prefix[0] = jnp.zeros((size, size), F32)
    u_copy.wait()
    v_copy.wait()
    for h in range(2):
        predict(1, h)
    panel_copies[1].wait_recv()
    for h in range(2):
        predict(near_window, h)
    x_copy.wait()

    for h in range(2):
        panel_copies[2 * h].wait_recv()
        predict(far_window, h)
        columns = slice(h * half, (h + 1) * half)

        def add_tile(i, sums):
            key = keys[i]
            t = jnp.bitwise_and(key, stride - 1)
            group = lax.shift_right_logical(key, stride.bit_length() - 1)
            col_mask = col_masks[t, :, columns]
            new = []
            for s, total in enumerate(sums):
                at = slice(s * strip, (s + 1) * strip)
                gap = x_buf[t, at, columns].astype(F32) - p_buf[h, group, at, :]
                residue = gap.astype(BF16) * (row_masks[t, at, :] * col_mask)
                new.append(total + residue.astype(F32))
                prefix[i + 1, at, columns] = new[-1]
            return tuple(new)

        zero = jnp.zeros((strip, half), F32)
        lax.fori_loop(0, slots, add_tile, (zero,) * (size // strip), unroll=4)

    def group_sum(r, window):
        group = r * 3 + window
        return prefix[bounds[group + 1]] - prefix[bounds[group]]

    for r in (1 - core, core):
        for window in range(3):
            total = group_sum(r, window)
            high = total.astype(BF16)
            columns = slice(window * size, (window + 1) * size)
            a_hi[r, :, columns] = high
            a_lo[r, :, columns] = (total - high.astype(F32)).astype(BF16)

    def products(r, columns, panel):
        return jnp.dot(a_hi[r, :, columns], panel, preferred_element_type=F32) + jnp.dot(
            a_lo[r, :, columns], panel, preferred_element_type=F32
        )

    t_copy.wait()
    panel_copies[4].wait_recv()
    first = near_window // 2
    pair = pl.ds(pl.multiple_of(first * size, size), 2 * size)
    panel = t_all[pl.ds(first, 2)].reshape(2 * size, size)
    for r in (1 - core, core):
        s_part[r] = products(r, pair, panel)
    panel_copies[3].wait_recv()

    def sketch_block(r):
        far = pl.ds(pl.multiple_of(far_window * size, size), size)
        return s_part[r] + products(r, far, t_all[far_window])

    step = size // CHUNKS
    half_send[...] = sketch_block(1 - core)
    half_copies = []
    for j in range(CHUNKS):
        at = pl.ds(j * step, step)
        half_copies.append(
            pltpu.make_async_remote_copy(
                src_ref=half_send.at[at],
                dst_ref=half_recv.at[at],
                send_sem=half_send_sem.at[j],
                recv_sem=half_recv_sem.at[j],
                device_id={"item": partner},
                device_id_type=MESH,
            )
        )
        half_copies[-1].start()
    own_half[...] = sketch_block(core)

    def part_copy(source_chip, at, send_sem, recv_sem, device):
        block = gathered.at[core, source_chip, at]
        copy = pltpu.make_async_remote_copy(
            src_ref=block,
            dst_ref=block,
            send_sem=send_sem,
            recv_sem=recv_sem,
            device_id={"item": device},
            device_id_type=MESH,
        )
        copy.start()
        return copy

    chip_copies = []
    pair_copies = [[] for _ in range(CHUNKS)]
    for j in range(CHUNKS):
        at = pl.ds(j * step, step)
        half_copies[j].wait_recv()
        gathered[core, chip, at, :] = (own_half[at, :] + half_recv[at, :]).astype(BF16)
        for d in range(1, chips):
            other = wrapped(chip + d, chips) * 2 + core
            sems = chip_send_sem.at[j, d - 1], chip_recv_sem.at[j, d - 1]
            chip_copies.append(part_copy(chip, at, *sems, other))
        sems = pair_send_sem.at[j, 0], pair_recv_sem.at[j, 0]
        pair_copies[j].append(part_copy(chip, at, *sems, partner))

    for r in range(blocks):
        for window in range(3):
            turned = group_sum(r, window).T
            high = turned.astype(BF16)
            at_both[r, window, :, :size] = high
            at_both[r, window, :, size:] = (turned - high.astype(F32)).astype(BF16)

    for j in range(CHUNKS):
        at = pl.ds(j * step, step)
        for d in range(1, chips):
            chip_copies[j * (chips - 1) + d - 1].wait_recv()
            sems = pair_send_sem.at[j, d], pair_recv_sem.at[j, d]
            source_chip = wrapped(chip + chips - d, chips)
            pair_copies[j].append(part_copy(source_chip, at, *sems, partner))

    def add_parts(r):
        total = gathered[r, 0].astype(F32)
        for other in range(1, chips):
            total = total + gathered[r, other].astype(F32)
        y_full[r] = total
        return total.astype(BF16)

    def second(r, window, y_half):
        return jnp.dot(
            at_both[r, window],
            jnp.concatenate([y_half, y_half], axis=0),
            preferred_element_type=F32,
        )

    y_half = add_parts(core)
    for window in range(3):
        z_part[window] = second(core, window, y_half)
    for j in range(CHUNKS):
        for copy in pair_copies[j]:
            copy.wait_recv()
    y_half = add_parts(1 - core)

    def term(window):
        return (z_part[window] + second(1 - core, window, y_half)).reshape(n_user, piece, size)

    piece = size // n_user
    turns = sorted(range(1, n_user), key=lambda d: -min(d, n_user - d)) + [0]
    far_send[...] = term(far_window).astype(far_send.dtype)
    z_copies = []
    for n, d in enumerate(turns):
        target = wrapped(user + d, n_user)
        z_copies.append(
            pltpu.make_async_remote_copy(
                src_ref=far_send.at[target],
                dst_ref=far_recv.at[target],
                send_sem=z_send_sem.at[n],
                recv_sem=z_recv_sem.at[n],
                device_id={"item": far_item},
                device_id_type=MESH,
            )
        )
        z_copies[-1].start()
    out_copy = pltpu.make_async_copy(y_full, sketch_out, local_sem.at[3])
    out_copy.start()
    near_send[...] = term(near_window)
    near_copy = pltpu.make_async_remote_copy(
        src_ref=near_send,
        dst_ref=near_recv,
        send_sem=z_send_sem.at[n_user],
        recv_sem=z_recv_sem.at[n_user],
        device_id={"item": partner},
        device_id_type=MESH,
    )
    near_copy.start()
    z_own[...] = term(1)

    near_copy.wait_recv()
    z_own[...] = z_own[...] + near_recv[...]
    piece_copies = []
    for n, d in enumerate(turns):
        target = wrapped(user + d, n_user)
        z_copies[n].wait_recv()
        total = z_own[target] + far_recv[target].astype(F32)
        if d == 0:
            piece_own[...] = total
            continue
        piece_send[target] = total.astype(piece_send.dtype)
        piece_copies.append(
            pltpu.make_async_remote_copy(
                src_ref=piece_send.at[target],
                dst_ref=piece_recv.at[n],
                send_sem=piece_send_sem.at[n],
                recv_sem=piece_recv_sem.at[n],
                device_id={"user": target},
                device_id_type=MESH,
            )
        )
        piece_copies[-1].start()
    total = piece_own[...]
    for n, copy in enumerate(piece_copies):
        copy.wait_recv()
        total = total + piece_recv[n].astype(F32)
    second_out[0] = total * scale

    out_copy.wait()
    for copy in panel_copies + half_copies + chip_copies + z_copies + [near_copy]:
        copy.wait_send()
    for copies in pair_copies:
        for copy in copies:
            copy.wait_send()
    for copy in piece_copies:
        copy.wait_send()


def hand_over(sketch, second, sketch_out, second_out, sem):
    copies = [
        pltpu.make_async_copy(second, second_out, sem.at[0]),
        pltpu.make_async_copy(sketch, sketch_out, sem.at[1]),
    ]
    for copy in copies:
        copy.start()
    for copy in copies:
        copy.wait()


def shards(
    xtiles, row_bits, col_bits, tile_row, tile_col, tile_count, user_panel, item_panel, test_panel
):
    size = item_panel.shape[0]
    slots = xtiles.shape[1]
    blocks = user_panel.shape[0] // size
    n_user, n_item = lax.axis_size("user"), lax.axis_size("item")
    chips = n_item // 2
    piece = size // n_user
    sent = BF16 if piece % 16 == 0 else F32
    scale = 2.0 / math.sqrt(n_user * slots * size)
    square = (size, size)
    words = row_bits.shape[2]
    dma = pltpu.SemaphoreType.DMA
    vmem = pl.BlockSpec(memory_space=pltpu.VMEM)
    hbm = pl.BlockSpec(memory_space=pltpu.HBM)
    sketch, second = pl.pallas_call(
        functools.partial(kernel, n_user, n_item, scale),
        out_shape=(
            pltpu.VMEM((blocks,) + square, F32),
            pltpu.VMEM((1, piece, size), F32),
        ),
        in_specs=[hbm] * 9,
        out_specs=(vmem, vmem),
        scratch_shapes=[
            pltpu.SMEM((1, words, slots), jnp.int32),
            pltpu.SMEM((1, words, slots), jnp.int32),
            pltpu.SMEM((1, slots), jnp.int32),
            pltpu.SMEM((1, slots), jnp.int32),
            pltpu.SMEM((1, 1), jnp.int32),
            pltpu.VMEM(user_panel.shape, BF16),
            pltpu.VMEM((slots,) + square, BF16),
            pltpu.VMEM((slots, size, size // 2), BF16),
            pltpu.VMEM((slots, 16, size), BF16),
            pltpu.VMEM((3,) + square, BF16),
            pltpu.VMEM((3,) + square, BF16),
            pltpu.VMEM((2, blocks * 3, size, size // 2), F32),
            pltpu.VMEM((slots + 1,) + square, F32),
            pltpu.SMEM((slots,), jnp.int32),
            pltpu.SMEM((blocks * 3 + 1,), jnp.int32),
            pltpu.VMEM((blocks, size, 3 * size), BF16),
            pltpu.VMEM((blocks, size, 3 * size), BF16),
            pltpu.VMEM((blocks, 3, size, 2 * size), BF16),
            pltpu.VMEM((blocks,) + square, F32),
            pltpu.VMEM(square, F32),
            pltpu.VMEM(square, F32),
            pltpu.VMEM(square, F32),
            pltpu.VMEM((blocks, chips) + square, BF16),
            pltpu.VMEM((blocks,) + square, F32),
            pltpu.VMEM((3,) + square, F32),
            pltpu.VMEM((n_user, piece, size), sent),
            pltpu.VMEM((n_user, piece, size), sent),
            pltpu.VMEM((n_user, piece, size), F32),
            pltpu.VMEM((n_user, piece, size), F32),
            pltpu.VMEM((n_user, piece, size), F32),
            pltpu.VMEM((piece, size), F32),
            pltpu.VMEM((n_user, piece, size), sent),
            pltpu.VMEM((n_user - 1, piece, size), sent),
            dma((10,)),
            dma((5,)),
            dma((5,)),
            dma((CHUNKS,)),
            dma((CHUNKS,)),
            dma((CHUNKS, chips - 1)),
            dma((CHUNKS, chips - 1)),
            dma((CHUNKS, chips)),
            dma((CHUNKS, chips)),
            dma((n_user + 1,)),
            dma((n_user + 1,)),
            dma((n_user - 1,)),
            dma((n_user - 1,)),
        ],
        compiler_params=pltpu.CompilerParams(
            collective_id=0, has_side_effects=True, vmem_limit_bytes=48 * 1024 * 1024
        ),
    )(
        *(
            operand
            if operand.size == 1
            else pltpu.with_memory_space_constraint(operand, pltpu.HBM)
            for operand in (
                jnp.swapaxes(row_bits, 1, 2),
                jnp.swapaxes(col_bits, 1, 2),
                tile_row,
                tile_col,
                tile_count,
                user_panel,
                xtiles,
                item_panel,
                test_panel,
            )
        )
    )
    sketch, second = pl.pallas_call(
        hand_over,
        out_shape=(
            jax.ShapeDtypeStruct(sketch.shape, F32),
            jax.ShapeDtypeStruct(second.shape, F32),
        ),
        in_specs=[vmem] * 2,
        out_specs=(hbm, hbm),
        scratch_shapes=[
            dma((2,)),
        ],
        compiler_params=pltpu.CompilerParams(vmem_limit_bytes=1024 * 1024),
    )(sketch, second)
    return sketch.reshape(blocks * size, size), second


def solution(mesh):
    placed = (
        P("user", "item", None, None),
        P("user", "item", None),
        P("user", "item", None),
        P("user", "item"),
        P("user", "item"),
        P("user", "item"),
        P("user", None),
        P("item", None),
        P("item", None),
    )
    return jax.shard_map(
        shards,
        mesh=mesh,
        in_specs=placed,
        out_specs=(P("user", None), P("item", "user", None)),
        check_vma=False,
    )
```
